256 devices in a mesh: grp: 8 (over y, core), sub: 32 (over x, z).
Axes of the slice: x: 4, y: 4, z: 8, core: 2. Of those that a mesh axis runs over, the one named last changes fastest.
Arguments:
- right_side: float32 [65536, 2048], P(('grp', 'sub'))
- schur: bfloat16 [131072, 512], P(('grp', 'sub'))
- inv_factor: bfloat16 [131072, 512], P(('grp', 'sub'))
- coarse_inverse: float32 [2048, 256], P('grp')
- primal_index: int32 [256, 8], P(('grp', 'sub')), may hold values from 0 to 255
- phase: int32 [65536], P(('grp', 'sub')), may hold values from 0 to 3
- phase_coef: float32 [4], replicated, may hold values from 0.5 to 4
Outputs:
- solution: float32 [65536, 2048], P(('grp', 'sub'))
- residual: float32 [65536, 2048], P(('grp', 'sub'))
The draws below stay inside these ranges and needn't reach their ends.
All inputs are finite; a program needn't handle non-finite values.
Results may differ from the reference program's by a relative error of at most 0.0056.
Values may be sent and summed in bfloat16 or wider, within the bound.
A program may use at most 64 MiB of HBM per device.

```python
import math
import jax
import jax.numpy as jnp
from jax import lax

NI = 512
NF = 256
NPD = 8
NC = 256
NRHS = 2048
PHASES = 4
SUBS = 256
ROWS = 65536
N_GRP = 8
N_SUB = 32


def draw_right_side(key, part):
    k1, k2, k3 = jax.random.split(key, 3)
    place = jnp.arange(ROWS, dtype=jnp.float32) / ROWS
    row_scale = (0.5 + place) * jnp.exp(jax.random.uniform(k1, (ROWS,), jnp.float32, -1.15, 1.15))
    col_scale = jnp.exp(jax.random.uniform(k2, (NRHS,), jnp.float32, -1.15, 1.15))
    base = jax.random.normal(k3, (ROWS, NRHS), jnp.float32)
    return (row_scale[:, None] * col_scale[None, :] * base).astype(jnp.float32)


def square_eye(width):
    return (jnp.arange(width)[:, None] == jnp.arange(width)[None, :]).astype(jnp.float32)


def draw_schur(key, part):
    k1, k2 = jax.random.split(jax.random.fold_in(key, 11))
    noise = jax.random.normal(k1, (SUBS, NI, NI), jnp.float32)
    sym = 0.6 * (noise + jnp.swapaxes(noise, 1, 2)) / jnp.sqrt(2.0 * NI)
    diag = jax.random.uniform(k2, (SUBS, NI, 1), jnp.float32, 1.5, 3.5)
    return (sym + diag * square_eye(NI)[None]).reshape(SUBS * NI, NI).astype(jnp.bfloat16)


def draw_inv_factor(key, part):
    k1, k2 = jax.random.split(jax.random.fold_in(key, 23))
    noise = 0.5 * jax.random.normal(k1, (SUBS, NI, NI), jnp.float32) / jnp.sqrt(1.0 * NI)
    diag = jax.random.uniform(k2, (SUBS, NI, 1), jnp.float32, 0.8, 1.6)
    return (noise + diag * square_eye(NI)[None]).reshape(SUBS * NI, NI).astype(jnp.bfloat16)


def draw_coarse_inverse(key, part):
    k1, k2, k3 = jax.random.split(jax.random.fold_in(key, 37), 3)
    noise = 0.5 * jax.random.normal(k1, (N_GRP, NC, NC), jnp.float32) / jnp.sqrt(1.0 * NC)
    diag = jax.random.uniform(k2, (N_GRP, NC, 1), jnp.float32, 0.5, 1.0)
    order = jax.random.permutation(k3, N_GRP).astype(jnp.float32)
    level = order / max(N_GRP - 1, 1)
    group_scale = jnp.exp(level * jnp.log(16.0))
    matrix = (noise + diag * square_eye(NC)[None]) * group_scale[:, None, None]
    return matrix.reshape(N_GRP * NC, NC).astype(jnp.float32)


def place_ends(drawn, rng, smallest, high):
    index_at = [jax.random.randint(jax.random.fold_in(rng, axis), (), 0, length) for axis, length in enumerate(drawn.shape)]
    main_axis = drawn.shape.index(max(drawn.shape))
    neighbour = index_at[:main_axis] + [(index_at[main_axis] + 1) % drawn.shape[main_axis]] + index_at[main_axis + 1:]
    return drawn.at[tuple(index_at)].set(smallest).at[tuple(neighbour)].set(high)


def setup_inputs(seed: int = 0) -> dict:
    key_of = jax.random.split(jax.random.key(seed), 8)
    return {
        "right_side": draw_right_side(jax.random.fold_in(key_of[7], 71), 0),
        "schur": draw_schur(jax.random.fold_in(key_of[7], 71), 0),
        "inv_factor": draw_inv_factor(jax.random.fold_in(key_of[7], 71), 0),
        "coarse_inverse": draw_coarse_inverse(jax.random.fold_in(key_of[7], 71), 0),
        "primal_index": place_ends(jax.random.randint(key_of[4], (SUBS, NPD), 0, NF), jax.random.fold_in(key_of[4], 1), 0, NF - 1).astype(jnp.int32),
        "phase": place_ends(jax.random.randint(key_of[5], (ROWS,), 0, PHASES), jax.random.fold_in(key_of[5], 1), 0, PHASES - 1).astype(jnp.int32),
        "phase_coef": jnp.clip(jnp.exp(jax.random.uniform(key_of[6], (PHASES,), jnp.float32, math.log(0.5), math.log(4.0))), 0.5, 4.0),
    }


def extend(block):
    return jnp.concatenate([jnp.roll(block, 1, axis=0), block], axis=1)


def assemble(local):
    return local[:, NF:, :] + jnp.roll(local[:, :NF, :], -1, axis=0)


def reference(right_side, schur, inv_factor, coarse_inverse, primal_index, phase, phase_coef):
    hi = lax.Precision.HIGHEST
    rhs = right_side.reshape(N_GRP, N_SUB, NF, NRHS)
    panels = schur.reshape(N_GRP, N_SUB, NI, NI)
    factors = inv_factor.reshape(N_GRP, N_SUB, NI, NI)
    coarse = coarse_inverse.reshape(N_GRP, NC, NC)
    picks = primal_index.reshape(N_GRP, N_SUB, NPD)
    labels = phase.reshape(N_GRP, N_SUB, NF)
    onehot = (picks[..., None] == jnp.arange(NF, dtype=jnp.int32)).astype(jnp.float32)
    coarse_rhs = jnp.einsum('gskf,gsfr->gskr', onehot, rhs, precision=hi).reshape(N_GRP, NC, NRHS)
    solved = jnp.einsum('gab,gbr->gar', coarse, coarse_rhs, precision=hi)
    shared = jnp.sum(solved, axis=0) / N_GRP
    correction = (solved + shared[None]).reshape(N_GRP, N_SUB, NPD, NRHS)
    table = (jnp.arange(PHASES, dtype=jnp.int32)[None, None, :] == labels[..., None]).astype(jnp.float32)
    coef_rows = jnp.einsum('gsfk,k->gsf', table, phase_coef, precision=hi)

    def one_group(items):
        rhs_g, panel_g, factor_g, onehot_g, corr_g, coef_g = items
        rb = rhs_g.astype(jnp.bfloat16)
        fac = factor_g.astype(jnp.float32)
        first = jnp.einsum('sij,sjr->sir', fac, extend(rb).astype(jnp.float32)).astype(jnp.bfloat16)
        second = jnp.einsum('sji,sjr->sir', fac, first.astype(jnp.float32)).astype(jnp.bfloat16)
        direction = 0.5 * assemble(second.astype(jnp.float32)) + jnp.einsum('skf,skr->sfr', onehot_g, corr_g, precision=hi)
        dirb = direction.astype(jnp.bfloat16)
        rz_group = jnp.sum(rhs_g * direction, axis=(0, 1))
        image = jnp.einsum('sij,sjr->sir', panel_g.astype(jnp.float32), extend(dirb).astype(jnp.float32)).astype(jnp.bfloat16)
        qvec = assemble(image.astype(jnp.float32)) + coef_g[..., None] * dirb.astype(jnp.float32)
        return dirb, qvec, rz_group

    dirb, qvec, rz_parts = lax.map(one_group, (rhs, panels, factors, onehot, correction, coef_rows))
    rz_total = jnp.sum(rz_parts, axis=0)
    pq_total = jnp.sum(dirb.astype(jnp.float32) * qvec, axis=(0, 1, 2))
    alpha = rz_total / pq_total
    solution = (alpha * dirb.astype(jnp.float32)).reshape(ROWS, NRHS)
    residual = (rhs - alpha * qvec).reshape(ROWS, NRHS)
    return solution, residual
```

```python
import functools

import jax
import jax.numpy as jnp
from jax import lax
from jax.experimental import pallas as pl
from jax.experimental.pallas import tpu as pltpu
from jax.sharding import PartitionSpec as P

MESH = pl.DeviceIdType.MESH
F32 = jnp.float32
BF16 = jnp.bfloat16
CHUNK = 256
LANES = 128


def plan(mesh, width, chunk):
    groups, subs = mesh.shape["grp"], mesh.shape["sub"]
    depth = 8 if subs >= 16 else 2
    chunks = width // chunk
    return dict(
        groups=groups,
        subs=subs,
        zs=depth,
        xs=subs // depth,
        chunk=chunk,
        chunks=chunks,
        per=chunk // LANES,
        blocks=width // LANES,
        stride=max(1, subs // (width // LANES)),
        late=2,
    )


def kernel(cfg, rs_hbm, s_hbm, g_hbm, k_hbm, idx_ref, phase_ref, table_ref, sol_hbm, res_hbm, sc):
    groups, subs, zs, xs = cfg["groups"], cfg["subs"], cfg["zs"], cfg["xs"]
    chunk, chunks, per = cfg["chunk"], cfg["chunks"], cfg["per"]
    blocks, stride, late = cfg["blocks"], cfg["stride"], cfg["late"]
    early = chunks - late
    face = rs_hbm.shape[0]
    prim = idx_ref.shape[1]
    g = lax.axis_index("grp")
    j = lax.axis_index("sub")
    x, z = j // zs, lax.rem(j, zs)
    right = lax.rem(j + 1, subs)
    left = lax.rem(j + subs - 1, subs)
    low = pl.ds(face, face)
    up = pl.ds(0, face)

    def remote(src, dst, ssem, rsem, where):
        return pltpu.make_async_remote_copy(
            src_ref=src, dst_ref=dst, send_sem=ssem, recv_sem=rsem, device_id=where, device_id_type=MESH
        )

    def drain(ref, sem):
        pltpu.make_async_copy(ref, ref, sem).wait()

    def cols(c):
        return pl.ds(pl.multiple_of(c * chunk, chunk), chunk)

    def load_rs(c):
        return pltpu.make_async_copy(rs_hbm.at[:, cols(c)], sc["rs"].at[c], sc["rs_sem"].at[c])

    load_g = pltpu.make_async_copy(g_hbm, sc["gm"], sc["mat_sem"].at[0])
    load_k = pltpu.make_async_copy(k_hbm, sc["km"], sc["mat_sem"].at[1])
    load_s = pltpu.make_async_copy(s_hbm, sc["sm"], sc["mat_sem"].at[2])

    def rb_copy(c):
        return remote(
            sc["ext"].at[c, low], sc["ext"].at[c, up], sc["rb_ss"].at[c], sc["rb_rs"].at[c], {"sub": right}
        )

    def v_copy(c):
        return remote(sc["v"].at[c, up], sc["vr"].at[c], sc["v_ss"].at[c], sc["v_rs"].at[c], {"sub": left})

    def zb_copy(c):
        return remote(
            sc["dir"].at[c, low], sc["dir"].at[c, up], sc["zb_ss"].at[c], sc["zb_rs"].at[c], {"sub": right}
        )

    def y_copy(c):
        return remote(sc["y"].at[c, up], sc["yr"].at[c], sc["y_ss"].at[c], sc["y_rs"].at[c], {"sub": left})

    for c in range(chunks):
        load_rs(c).start()
    load_g.start()
    load_k.start()
    load_s.start()
    barrier = pltpu.get_barrier_semaphore()

    def greet_sub(d, carry):
        pl.semaphore_signal(barrier, inc=1, device_id={"sub": lax.rem(j + d, subs)}, device_id_type=MESH)
        return carry

    def greet_grp(d, carry):
        pl.semaphore_signal(barrier, inc=1, device_id={"grp": lax.rem(g + d, groups)}, device_id_type=MESH)
        return carry

    lax.fori_loop(1, subs, greet_sub, 0)
    lax.fori_loop(1, groups, greet_grp, 0)

    def cast(c):
        load_rs(c).wait()
        sc["ext"][c, low, :] = sc["rs"][c].astype(BF16)

    cast(0)
    pl.semaphore_wait(barrier, subs - 1 + groups - 1)
    rb_copy(0).start()

    def cast_rest(c, carry):
        cast(c)
        return carry

    def cast_send(c, carry):
        cast(c)
        rb_copy(c).start()
        return carry

    ahead = min(cfg.get("ahead", 3), chunks)
    lax.fori_loop(1, ahead, cast_send, 0)
    lax.fori_loop(ahead, chunks, cast_rest, 0)

    def pick(c, carry):
        for k in range(prim):
            row = sc["rs"][c, pl.ds(idx_ref[0, k], 1), :]
            for h in range(per):
                sc["rc"][c * per + h, k : k + 1, :] = row[:, h * LANES : (h + 1) * LANES]
        return carry

    lax.fori_loop(0, chunks, pick, 0)

    def rc_copy(b):
        return remote(
            sc["rc"].at[b], sc["rcin"].at[j], sc["rc_ss"].at[b], sc["rc_rs"], {"sub": b * stride}
        )

    def rc_send(b, carry):
        @pl.when(b * stride != j)
        def _():
            rc_copy(b).start()

        @pl.when(b * stride == j)
        def _():
            sc["rcin"][j] = sc["rc"][b]

        return carry

    lax.fori_loop(0, blocks, rc_send, 0)

    load_g.wait()
    sc["gt"][...] = sc["gm"][...].T
    lane = lax.broadcasted_iota(jnp.int32, (4 * prim, face), 1)
    sub_i = lax.broadcasted_iota(jnp.int32, (4 * prim, face), 0)
    which = jnp.full((4 * prim, face), -1, jnp.int32)
    for k in range(prim):
        which = jnp.where(lax.rem(sub_i, prim) == k, idx_ref[0, k], which)
    hot = jnp.where((lane == which) & (sub_i < 3 * prim), 1.0, 0.0).astype(F32)
    sc["pt"][...] = hot.T.astype(BF16)
    labels = phase_ref[...]
    coef = jnp.zeros(labels.shape, F32)
    for k in range(table_ref.shape[0]):
        coef = jnp.where(labels == k, table_ref[k], coef)
    sc["coef"][...] = jnp.broadcast_to(coef, (LANES, face)).T
    sc["ra"][...] = jnp.zeros_like(sc["ra"])

    def first(c, carry):
        rb_copy(c).wait_recv()

        @pl.when(c + ahead < chunks)
        def _():
            rb_copy(c + ahead).start()

        u = jnp.dot(sc["gm"][...], sc["ext"][c], preferred_element_type=F32).astype(BF16)
        sc["v"][c] = jnp.dot(sc["gt"][...], u, preferred_element_type=F32).astype(BF16)
        v_copy(c).start()
        return carry

    is_solver = (lax.rem(j, stride) == 0) & (j < blocks * stride)
    my_block = j // stride

    def h_copy(t):
        return remote(
            sc["hout"].at[t], sc["hin"].at[my_block], sc["h_ss"].at[t], sc["h_rs"], {"sub": t}
        )

    def solve():
        @pl.when(is_solver)
        def _():
            load_k.wait()
            drain(sc["rcin"].at[pl.ds(0, subs - 1)], sc["rc_rs"])
            rhs = sc["rcin"][...].reshape(subs * prim, LANES)
            h = jnp.dot(sc["km"][...], rhs, precision=lax.Precision.HIGHEST, preferred_element_type=F32)
            sc["hout"][...] = h.reshape(subs, prim, LANES)

            def h_send(d, carry):
                h_copy(lax.rem(j + d, subs)).start()
                return carry

            lax.fori_loop(1, subs, h_send, 0)
            sc["hin"][my_block] = sc["hout"][j]

        @pl.when(jnp.logical_not(is_solver))
        def _():
            load_k.wait()

    def g_copy(t):
        return remote(sc["hin"], sc["gin"].at[g], sc["g_ss"].at[t], sc["g_rs"], {"grp": t})

    def share():
        @pl.when(is_solver)
        def _():
            drain(sc["hin"].at[pl.ds(0, blocks - 1)], sc["h_rs"])

        @pl.when(jnp.logical_not(is_solver))
        def _():
            drain(sc["hin"], sc["h_rs"])

        def g_send(d, carry):
            g_copy(lax.rem(g + d, groups)).start()
            return carry

        lax.fori_loop(1, groups, g_send, 0)
        sc["gin"][g] = sc["hin"][...]

    def correct():
        drain(sc["gin"].at[pl.ds(0, groups - 1)], sc["g_rs"])
        for b in range(blocks):
            total = sc["gin"][0, b]
            for t in range(1, groups):
                total = total + sc["gin"][t, b]
            e = sc["hin"][b] + total / groups
            hi = e.astype(BF16).astype(F32)
            rest = e - hi
            mid = rest.astype(BF16).astype(F32)
            tail = rest - mid
            c, h = divmod(b, per)
            stack = jnp.concatenate([hi, mid, tail, jnp.zeros_like(hi)], axis=0)
            sc["e3"][c, :, h * LANES : (h + 1) * LANES] = stack.astype(BF16)

    def rows_to(ref, base, c, value):
        for h in range(per):
            ref[base + c * per + h] = value[:, h * LANES : (h + 1) * LANES]

    def direction(c, carry):
        v_copy(c).wait_recv()
        fix = jnp.dot(sc["pt"][...], sc["e3"][c], preferred_element_type=F32)
        both = sc["v"][c, low, :].astype(F32) + sc["vr"][c].astype(F32)
        zz = 0.5 * both + fix
        sc["dir"][c, low, :] = zz.astype(BF16)
        zb_copy(c).start()
        rows_to(sc["ra"], 0, c, jnp.sum(sc["rs"][c] * zz, axis=0, keepdims=True))
        return carry

    def wide_coef():
        return jnp.concatenate([sc["coef"][...]] * per, axis=1)

    def image(c, ref, base):
        zb_copy(c).wait_recv()
        y = jnp.dot(sc["sm"][...], sc["dir"][c], preferred_element_type=F32).astype(BF16)
        sc["y"][c] = y
        y_copy(c).start()
        zf = sc["dir"][c, low, :].astype(F32)
        part = jnp.sum(sc["dir"][c].astype(F32) * sc["y"][c].astype(F32), axis=0, keepdims=True)
        part = part + jnp.sum(wide_coef() * zf * zf, axis=0, keepdims=True)
        rows_to(ref, base, c, part)

    def finish(c, carry):
        y_copy(c).wait_recv()
        alpha = jnp.concatenate([sc["alpha"][c * per + h] for h in range(per)], axis=1)
        zf = sc["dir"][c, low, :].astype(F32)
        q = sc["y"][c, low, :].astype(F32) + sc["yr"][c].astype(F32) + wide_coef() * zf
        sc["sol"][c] = alpha * zf
        out_sol(c).start()
        sc["res"][c] = sc["rs"][c] - alpha * q
        out_res(c).start()
        return carry

    def out_sol(c):
        return pltpu.make_async_copy(sc["sol"].at[c], sol_hbm.at[:, cols(c)], sc["os"].at[c])

    def out_res(c):
        return pltpu.make_async_copy(sc["res"].at[c], res_hbm.at[:, cols(c)], sc["or"].at[c])

    span = sc["ra"].shape[0] // groups

    def exchange(name, count, me, where, src_of):
        def copy(t):
            return remote(src_of(t), sc[name].at[me], sc[name + "_ss"].at[t], sc[name + "_rs"], where(t))

        def start(own):
            def go(d, carry):
                copy(lax.rem(me + d, count)).start()
                return carry

            lax.fori_loop(1, count, go, 0)
            sc[name][me] = own

        def end():
            drain(sc[name].at[pl.ds(0, count - 1)], sc[name + "_rs"])
            total = sc[name][0]
            for t in range(1, count):
                total = total + sc[name][t]
            return total

        def sent():
            def go(d, carry):
                copy(lax.rem(me + d, count)).wait_send()
                return carry

            lax.fori_loop(1, count, go, 0)

        return start, end, sent

    to_grp = lambda t: {"grp": t}
    to_x = lambda t: {"sub": t * zs + z}
    to_z = lambda t: {"sub": x * zs + t}
    a1 = exchange("a1", groups, g, to_grp, lambda t: sc["ra"].at[pl.ds(t * span, span)])
    a2 = exchange("a2", xs, x, to_x, lambda t: sc["a2o"])
    a3 = exchange("a3", zs, z, to_z, lambda t: sc["a3o"])
    a4 = exchange("a4", groups, g, to_grp, lambda t: sc["a4o"])
    b1 = exchange("b1", groups, g, to_grp, lambda t: sc["rbt"])
    b2 = exchange("b2", xs, x, to_x, lambda t: sc["b2o"])
    b3 = exchange("b3", zs, z, to_z, lambda t: sc["b3o"])

    def hop(before, after, name):
        total = before[1]()
        sc[name][...] = total
        after[0](total)

    lax.fori_loop(0, chunks // 4, first, 0)
    solve()
    lax.fori_loop(chunks // 4, chunks // 2, first, 0)
    share()
    lax.fori_loop(chunks // 2, 3 * chunks // 4, first, 0)
    correct()
    lead = chunks - 3 * chunks // 4

    def first_dir(c, carry):
        direction(c - 3 * chunks // 4, 0)
        first(c, 0)
        return carry

    lax.fori_loop(3 * chunks // 4, chunks, first_dir, 0)
    load_s.wait()
    base = chunks * per

    def dir_image(c, carry):
        direction(c + lead, 0)
        image(c, sc["ra"], base)
        return carry

    lax.fori_loop(0, chunks - lead, dir_image, 0)
    for c in range(chunks - lead, early):
        image(c, sc["ra"], base)
    a1[0](sc["ra"][pl.ds(g * span, span)])
    for i in range(late):
        image(early + i, sc["rbt"], -early * per)
        if i == 0:
            hop(a1, a2, "a2o")
    b1[0](sc["rbt"][...])
    hop(a2, a3, "a3o")
    hop(b1, b2, "b2o")
    hop(a3, a4, "a4o")
    hop(b2, b3, "b3o")
    drain(sc["a4"].at[pl.ds(0, groups - 1)], sc["a4_rs"])
    for r in range(early * per):
        n, d = r, base + r
        sc["alpha"][r] = sc["a4"][n // span, n % span] / sc["a4"][d // span, d % span]
    lax.fori_loop(0, early, finish, 0)
    last = b3[1]()
    for r in range(late * per):
        n = early * per + r
        sc["alpha"][n] = sc["a4"][n // span, n % span] / last[r]
    lax.fori_loop(early, chunks, finish, 0)

    def drain_streams(c, carry):
        rb_copy(c).wait_send()
        v_copy(c).wait_send()
        zb_copy(c).wait_send()
        y_copy(c).wait_send()
        return carry

    lax.fori_loop(0, chunks, drain_streams, 0)

    def drain_rc(b, carry):
        @pl.when(b * stride != j)
        def _():
            rc_copy(b).wait_send()

        return carry

    lax.fori_loop(0, blocks, drain_rc, 0)

    @pl.when(is_solver)
    def _():
        def drain_h(d, carry):
            h_copy(lax.rem(j + d, subs)).wait_send()
            return carry

        lax.fori_loop(1, subs, drain_h, 0)

    def drain_g(d, carry):
        g_copy(lax.rem(g + d, groups)).wait_send()
        return carry

    lax.fori_loop(1, groups, drain_g, 0)
    for stage in (a1, a2, a3, a4, b1, b2, b3):
        stage[2]()

    def drain_out(c, carry):
        out_sol(c).wait()
        out_res(c).wait()
        return carry

    lax.fori_loop(0, chunks, drain_out, 0)


def scratch(cfg, face, prim):
    n, chunk, per = cfg["chunks"], cfg["chunk"], cfg["per"]
    groups, subs, xs, zs, blocks = cfg["groups"], cfg["subs"], cfg["xs"], cfg["zs"], cfg["blocks"]
    rows_a = (2 * n - cfg["late"]) * per
    span = -(-rows_a // groups)
    rows_b = cfg["late"] * per
    vm, dma = pltpu.VMEM, pltpu.SemaphoreType.DMA
    out = dict(
        rs=vm((n, face, chunk), F32),
        ext=vm((n, 2 * face, chunk), BF16),
        v=vm((n, 2 * face, chunk), BF16),
        vr=vm((n, face, chunk), BF16),
        dir=vm((n, 2 * face, chunk), BF16),
        y=vm((n, 2 * face, chunk), BF16),
        yr=vm((n, face, chunk), BF16),
        sol=vm((n, face, chunk), F32),
        res=vm((n, face, chunk), F32),
        gm=vm((2 * face, 2 * face), BF16),
        gt=vm((2 * face, 2 * face), BF16),
        sm=vm((2 * face, 2 * face), BF16),
        km=vm((subs * prim, subs * prim), F32),
        pt=vm((face, 4 * prim), BF16),
        coef=vm((face, LANES), F32),
        rc=vm((blocks, prim, LANES), F32),
        rcin=vm((subs, prim, LANES), F32),
        hout=vm((subs, prim, LANES), F32),
        hin=vm((blocks, prim, LANES), F32),
        gin=vm((groups, blocks, prim, LANES), F32),
        e3=vm((n, 4 * prim, chunk), BF16),
        alpha=vm((n * per, 1, LANES), F32),
        ra=vm((span * groups, 1, LANES), F32),
        rbt=vm((rows_b, 1, LANES), F32),
        a1=vm((groups, span, 1, LANES), F32),
        a2=vm((xs, span, 1, LANES), F32),
        a3=vm((zs, span, 1, LANES), F32),
        a4=vm((groups, span, 1, LANES), F32),
        a2o=vm((span, 1, LANES), F32),
        a3o=vm((span, 1, LANES), F32),
        a4o=vm((span, 1, LANES), F32),
        b1=vm((groups, rows_b, 1, LANES), F32),
        b2=vm((xs, rows_b, 1, LANES), F32),
        b3=vm((zs, rows_b, 1, LANES), F32),
        b2o=vm((rows_b, 1, LANES), F32),
        b3o=vm((rows_b, 1, LANES), F32),
        rs_sem=dma((n,)),
        mat_sem=dma((3,)),
        rc_ss=dma((blocks,)),
        rc_rs=dma(()),
        h_ss=dma((subs,)),
        h_rs=dma(()),
        g_ss=dma((groups,)),
        g_rs=dma(()),
        os=dma((n,)),
    )
    out["or"] = dma((n,))
    for name in ("rb", "v", "zb", "y"):
        out[name + "_ss"] = dma((n,))
        out[name + "_rs"] = dma((n,))
    for name, count in (("a1", groups), ("a2", xs), ("a3", zs), ("a4", groups), ("b1", groups), ("b2", xs), ("b3", zs)):
        out[name + "_ss"] = dma((count,))
        out[name + "_rs"] = dma(())
    return out


def solution(mesh, chunk=CHUNK):
    def body(right_side, schur, inv_factor, coarse_inverse, primal_index, phase, phase_coef):
        face, width = right_side.shape
        cfg = plan(mesh, width, chunk)
        shapes = scratch(cfg, face, primal_index.shape[1])
        keys = list(shapes)

        def wrapped(*refs):
            kernel(cfg, *refs[:9], dict(zip(keys, refs[9:])))

        anyspace = pl.BlockSpec(memory_space=pl.ANY)
        smem = pl.BlockSpec(memory_space=pltpu.SMEM)
        vmem = pl.BlockSpec(memory_space=pltpu.VMEM)
        out = jax.ShapeDtypeStruct((face, width), F32)
        return pl.pallas_call(
            wrapped,
            out_shape=(out, out),
            in_specs=[anyspace] * 4 + [smem, vmem, smem],
            out_specs=(anyspace, anyspace),
            scratch_shapes=[shapes[k] for k in keys],
            compiler_params=pltpu.CompilerParams(
                collective_id=0, has_side_effects=True, vmem_limit_bytes=44 * 1024 * 1024
            ),
            name="bddc_step",
        )(right_side, schur, inv_factor, coarse_inverse, primal_index, phase.reshape(1, face), phase_coef)

    both = ("grp", "sub")
    in_specs = (
        P(both, None),
        P(both, None),
        P(both, None),
        P("grp", None),
        P(both, None),
        P(both),
        P(),
    )
    out_specs = (P(both, None), P(both, None))
    return jax.shard_map(body, mesh=mesh, in_specs=in_specs, out_specs=out_specs, check_vma=False)
```

```python
import functools

import jax
import jax.numpy as jnp
from jax import lax
from jax.experimental import pallas as pl
from jax.experimental.pallas import tpu as pltpu
from jax.sharding import PartitionSpec as P

MESH = pl.DeviceIdType.MESH
F32 = jnp.float32
BF16 = jnp.bfloat16
CHUNK = 256
LANES = 128


def plan(mesh, width, chunk):
    groups, subs = mesh.shape["grp"], mesh.shape["sub"]
    depth = 8 if subs >= 16 else 2
    chunks = width // chunk
    return dict(
        groups=groups,
        subs=subs,
        zs=depth,
        xs=subs // depth,
        chunk=chunk,
        chunks=chunks,
        per=chunk // LANES,
        blocks=width // LANES,
        stride=max(1, subs // (width // LANES)),
        late=2,
    )


def kernel(cfg, rs_hbm, s_hbm, g_hbm, k_hbm, idx_hbm, phase_hbm, table_hbm, sol_ref, res_ref, sc):
    groups, subs, zs, xs = cfg["groups"], cfg["subs"], cfg["zs"], cfg["xs"]
    chunk, chunks, per = cfg["chunk"], cfg["chunks"], cfg["per"]
    blocks, stride, late = cfg["blocks"], cfg["stride"], cfg["late"]
    early = chunks - late
    face = rs_hbm.shape[0]
    prim = idx_hbm.shape[1]
    idx_ref, phase_ref, table_ref = sc["idx"], sc["phase"], sc["table"]
    g = lax.axis_index("grp")
    j = lax.axis_index("sub")
    x, z = j // zs, lax.rem(j, zs)
    right = lax.rem(j + 1, subs)
    left = lax.rem(j + subs - 1, subs)
    low = pl.ds(face, face)
    up = pl.ds(0, face)

    def remote(src, dst, ssem, rsem, where):
        return pltpu.make_async_remote_copy(
            src_ref=src, dst_ref=dst, send_sem=ssem, recv_sem=rsem, device_id=where, device_id_type=MESH
        )

    def drain(ref, sem):
        pltpu.make_async_copy(ref, ref, sem).wait()

    def cols(c):
        return pl.ds(pl.multiple_of(c * chunk, chunk), chunk)

    def load_rs(c):
        return pltpu.make_async_copy(rs_hbm.at[:, cols(c)], sc["rs"].at[c], sc["rs_sem"].at[c])

    load_g = pltpu.make_async_copy(g_hbm, sc["gm"], sc["mat_sem"].at[0])
    load_k = pltpu.make_async_copy(k_hbm, sc["km"], sc["mat_sem"].at[1])
    load_s = pltpu.make_async_copy(s_hbm, sc["sm"], sc["mat_sem"].at[2])

    def rb_copy(c):
        return remote(
            sc["ext"].at[c, low], sc["ext"].at[c, up], sc["rb_ss"].at[c], sc["rb_rs"].at[c], {"sub": right}
        )

    def v_copy(c):
        return remote(sc["v"].at[c, up], sc["vr"].at[c], sc["v_ss"].at[c], sc["v_rs"].at[c], {"sub": left})

    def zb_copy(c):
        return remote(
            sc["dir"].at[c, low], sc["dir"].at[c, up], sc["zb_ss"].at[c], sc["zb_rs"].at[c], {"sub": right}
        )

    def y_copy(c):
        return remote(sc["y"].at[c, up], sc["yr"].at[c], sc["y_ss"].at[c], sc["y_rs"].at[c], {"sub": left})

    small = [
        pltpu.make_async_copy(idx_hbm, idx_ref, sc["mat_sem"].at[3]),
        pltpu.make_async_copy(phase_hbm, phase_ref, sc["mat_sem"].at[4]),
        pltpu.make_async_copy(table_hbm, table_ref, sc["mat_sem"].at[5]),
    ]

    for c in range(chunks):
        load_rs(c).start()
    for load in small:
        load.start()
    load_g.start()
    load_k.start()
    load_s.start()
    barrier = pltpu.get_barrier_semaphore()

    def greet_sub(d, carry):
        pl.semaphore_signal(barrier, inc=1, device_id={"sub": lax.rem(j + d, subs)}, device_id_type=MESH)
        return carry

    def greet_grp(d, carry):
        pl.semaphore_signal(barrier, inc=1, device_id={"grp": lax.rem(g + d, groups)}, device_id_type=MESH)
        return carry

    lax.fori_loop(1, subs, greet_sub, 0)
    lax.fori_loop(1, groups, greet_grp, 0)

    def cast(c):
        load_rs(c).wait()
        sc["ext"][c, low, :] = sc["rs"][c].astype(BF16)

    cast(0)
    pl.semaphore_wait(barrier, subs - 1 + groups - 1)
    rb_copy(0).start()

    def cast_rest(c, carry):
        cast(c)
        return carry

    def cast_send(c, carry):
        cast(c)
        rb_copy(c).start()
        return carry

    ahead = min(cfg.get("ahead", 2), chunks)
    lax.fori_loop(1, ahead, cast_send, 0)
    lax.fori_loop(ahead, chunks, cast_rest, 0)

    def pick(c, carry):
        for k in range(prim):
            row = sc["rs"][c, pl.ds(idx_ref[0, k], 1), :]
            for h in range(per):
                sc["rc"][c * per + h, k : k + 1, :] = row[:, h * LANES : (h + 1) * LANES]
        return carry

    for load in small:
        load.wait()
    lax.fori_loop(0, chunks, pick, 0)

    def rc_copy(b):
        return remote(
            sc["rc"].at[b], sc["rcin"].at[j], sc["rc_ss"].at[b], sc["rc_rs"], {"sub": b * stride}
        )

    def rc_send(b, carry):
        @pl.when(b * stride != j)
        def _():
            rc_copy(b).start()

        @pl.when(b * stride == j)
        def _():
            sc["rcin"][j] = sc["rc"][b]

        return carry

    lax.fori_loop(0, blocks, rc_send, 0)

    load_g.wait()
    sc["gt"][...] = sc["gm"][...].T
    lane = lax.broadcasted_iota(jnp.int32, (4 * prim, face), 1)
    sub_i = lax.broadcasted_iota(jnp.int32, (4 * prim, face), 0)
    which = jnp.full((4 * prim, face), -1, jnp.int32)
    for k in range(prim):
        which = jnp.where(lax.rem(sub_i, prim) == k, idx_ref[0, k], which)
    hot = jnp.where((lane == which) & (sub_i < 3 * prim), 1.0, 0.0).astype(F32)
    sc["pt"][...] = hot.T.astype(BF16)
    labels = phase_ref[...]
    coef = jnp.zeros(labels.shape, F32)
    for k in range(table_ref.shape[1]):
        coef = jnp.where(labels == k, table_ref[0, k], coef)
    sc["coef"][...] = jnp.broadcast_to(coef, (LANES, face)).T
    sc["ra"][...] = jnp.zeros_like(sc["ra"])

    def first(c, carry):
        rb_copy(c).wait_recv()

        @pl.when(c + ahead < chunks)
        def _():
            rb_copy(c + ahead).start()

        u = jnp.dot(sc["gm"][...], sc["ext"][c], preferred_element_type=F32).astype(BF16)
        sc["v"][c] = jnp.dot(sc["gt"][...], u, preferred_element_type=F32).astype(BF16)
        v_copy(c).start()
        return carry

    is_solver = (lax.rem(j, stride) == 0) & (j < blocks * stride)
    my_block = j // stride

    def h_copy(t):
        return remote(
            sc["hout"].at[t], sc["hin"].at[my_block], sc["h_ss"].at[t], sc["h_rs"], {"sub": t}
        )

    def solve():
        @pl.when(is_solver)
        def _():
            load_k.wait()
            drain(sc["rcin"].at[pl.ds(0, subs - 1)], sc["rc_rs"])
            rhs = sc["rcin"][...].reshape(subs * prim, LANES)
            h = jnp.dot(sc["km"][...], rhs, precision=lax.Precision.HIGHEST, preferred_element_type=F32)
            sc["hout"][...] = h.reshape(subs, prim, LANES)

            def h_send(d, carry):
                h_copy(lax.rem(j + d, subs)).start()
                return carry

            lax.fori_loop(1, subs, h_send, 0)
            sc["hin"][my_block] = sc["hout"][j]

        @pl.when(jnp.logical_not(is_solver))
        def _():
            load_k.wait()

    def g_copy(t):
        return remote(sc["hin"], sc["gin"].at[g], sc["g_ss"].at[t], sc["g_rs"], {"grp": t})

    def share():
        @pl.when(is_solver)
        def _():
            drain(sc["hin"].at[pl.ds(0, blocks - 1)], sc["h_rs"])

        @pl.when(jnp.logical_not(is_solver))
        def _():
            drain(sc["hin"], sc["h_rs"])

        def g_send(d, carry):
            g_copy(lax.rem(g + d, groups)).start()
            return carry

        lax.fori_loop(1, groups, g_send, 0)
        sc["gin"][g] = sc["hin"][...]

    def correct():
        drain(sc["gin"].at[pl.ds(0, groups - 1)], sc["g_rs"])
        for b in range(blocks):
            total = sc["gin"][0, b]
            for t in range(1, groups):
                total = total + sc["gin"][t, b]
            e = sc["hin"][b] + total / groups
            hi = e.astype(BF16).astype(F32)
            rest = e - hi
            mid = rest.astype(BF16).astype(F32)
            tail = rest - mid
            c, h = divmod(b, per)
            stack = jnp.concatenate([hi, mid, tail, jnp.zeros_like(hi)], axis=0)
            sc["e3"][c, :, h * LANES : (h + 1) * LANES] = stack.astype(BF16)

    def rows_to(ref, base, c, value):
        for h in range(per):
            ref[base + c * per + h] = value[:, h * LANES : (h + 1) * LANES]

    def direction(c, carry):
        v_copy(c).wait_recv()
        fix = jnp.dot(sc["pt"][...], sc["e3"][c], preferred_element_type=F32)
        both = sc["v"][c, low, :].astype(F32) + sc["vr"][c].astype(F32)
        zz = 0.5 * both + fix
        sc["dir"][c, low, :] = zz.astype(BF16)
        zb_copy(c).start()
        rows_to(sc["ra"], 0, c, jnp.sum(sc["rs"][c] * zz, axis=0, keepdims=True))
        return carry

    def wide_coef():
        return jnp.concatenate([sc["coef"][...]] * per, axis=1)

    def image(c, ref, base):
        zb_copy(c).wait_recv()
        y = jnp.dot(sc["sm"][...], sc["dir"][c], preferred_element_type=F32).astype(BF16)
        sc["y"][c] = y
        y_copy(c).start()
        zf = sc["dir"][c, low, :].astype(F32)
        part = jnp.sum(sc["dir"][c].astype(F32) * sc["y"][c].astype(F32), axis=0, keepdims=True)
        part = part + jnp.sum(wide_coef() * zf * zf, axis=0, keepdims=True)
        rows_to(ref, base, c, part)

    def finish(c, carry):
        y_copy(c).wait_recv()
        alpha = jnp.concatenate([sc["alpha"][c * per + h] for h in range(per)], axis=1)
        zf = sc["dir"][c, low, :].astype(F32)
        q = sc["y"][c, low, :].astype(F32) + sc["yr"][c].astype(F32) + wide_coef() * zf
        sol_ref[:, cols(c)] = alpha * zf
        res_ref[:, cols(c)] = sc["rs"][c] - alpha * q
        return carry

    span = sc["ra"].shape[0] // groups

    def exchange(name, count, me, where, src_of):
        def copy(t):
            return remote(src_of(t), sc[name].at[me], sc[name + "_ss"].at[t], sc[name + "_rs"], where(t))

        def start(own):
            def go(d, carry):
                copy(lax.rem(me + d, count)).start()
                return carry

            lax.fori_loop(1, count, go, 0)
            sc[name][me] = own

        def end():
            drain(sc[name].at[pl.ds(0, count - 1)], sc[name + "_rs"])
            total = sc[name][0]
            for t in range(1, count):
                total = total + sc[name][t]
            return total

        def sent():
            def go(d, carry):
                copy(lax.rem(me + d, count)).wait_send()
                return carry

            lax.fori_loop(1, count, go, 0)

        return start, end, sent

    to_grp = lambda t: {"grp": t}
    to_x = lambda t: {"sub": t * zs + z}
    to_z = lambda t: {"sub": x * zs + t}
    a1 = exchange("a1", groups, g, to_grp, lambda t: sc["ra"].at[pl.ds(t * span, span)])
    a2 = exchange("a2", xs, x, to_x, lambda t: sc["a2o"])
    a3 = exchange("a3", zs, z, to_z, lambda t: sc["a3o"])
    a4 = exchange("a4", groups, g, to_grp, lambda t: sc["a4o"])
    b1 = exchange("b1", groups, g, to_grp, lambda t: sc["rbt"])
    b2 = exchange("b2", subs, j, lambda t: {"sub": t}, lambda t: sc["b2o"])

    def hop(before, after, name):
        total = before[1]()
        sc[name][...] = total
        after[0](total)

    lax.fori_loop(0, chunks // 4, first, 0)
    solve()
    lax.fori_loop(chunks // 4, chunks // 2, first, 0)
    share()
    lax.fori_loop(chunks // 2, 3 * chunks // 4, first, 0)
    correct()
    lead = chunks - 3 * chunks // 4

    def first_dir(c, carry):
        direction(c - 3 * chunks // 4, 0)
        first(c, 0)
        return carry

    lax.fori_loop(3 * chunks // 4, chunks, first_dir, 0)
    load_s.wait()
    base = chunks * per

    def dir_image(c, carry):
        direction(c + lead, 0)
        image(c, sc["ra"], base)
        return carry

    lax.fori_loop(0, chunks - lead, dir_image, 0)
    for c in range(chunks - lead, early):
        image(c, sc["ra"], base)
    a1[0](sc["ra"][pl.ds(g * span, span)])
    for i in range(late):
        image(early + i, sc["rbt"], -early * per)
        if i == 0:
            hop(a1, a2, "a2o")
    b1[0](sc["rbt"][...])
    hop(a2, a3, "a3o")
    hop(b1, b2, "b2o")
    hop(a3, a4, "a4o")
    drain(sc["a4"].at[pl.ds(0, groups - 1)], sc["a4_rs"])
    for r in range(early * per):
        n, d = r, base + r
        sc["alpha"][r] = sc["a4"][n // span, n % span] / sc["a4"][d // span, d % span]
    lax.fori_loop(0, early, finish, 0)
    last = b2[1]()
    for r in range(late * per):
        n = early * per + r
        sc["alpha"][n] = sc["a4"][n // span, n % span] / last[r]
    lax.fori_loop(early, chunks, finish, 0)

    def drain_streams(c, carry):
        rb_copy(c).wait_send()
        v_copy(c).wait_send()
        zb_copy(c).wait_send()
        y_copy(c).wait_send()
        return carry

    lax.fori_loop(0, chunks, drain_streams, 0)

    def drain_rc(b, carry):
        @pl.when(b * stride != j)
        def _():
            rc_copy(b).wait_send()

        return carry

    lax.fori_loop(0, blocks, drain_rc, 0)

    @pl.when(is_solver)
    def _():
        def drain_h(d, carry):
            h_copy(lax.rem(j + d, subs)).wait_send()
            return carry

        lax.fori_loop(1, subs, drain_h, 0)

    def drain_g(d, carry):
        g_copy(lax.rem(g + d, groups)).wait_send()
        return carry

    lax.fori_loop(1, groups, drain_g, 0)
    for stage in (a1, a2, a3, a4, b1, b2):
        stage[2]()


def scratch(cfg, face, prim, phases):
    n, chunk, per = cfg["chunks"], cfg["chunk"], cfg["per"]
    groups, subs, xs, zs, blocks = cfg["groups"], cfg["subs"], cfg["xs"], cfg["zs"], cfg["blocks"]
    rows_a = (2 * n - cfg["late"]) * per
    span = -(-rows_a // groups)
    rows_b = cfg["late"] * per
    vm, dma = pltpu.VMEM, pltpu.SemaphoreType.DMA
    out = dict(
        rs=vm((n, face, chunk), F32),
        ext=vm((n, 2 * face, chunk), BF16),
        v=vm((n, 2 * face, chunk), BF16),
        vr=vm((n, face, chunk), BF16),
        dir=vm((n, 2 * face, chunk), BF16),
        y=vm((n, 2 * face, chunk), BF16),
        yr=vm((n, face, chunk), BF16),
        idx=pltpu.SMEM((1, prim), jnp.int32),
        phase=vm((1, face), jnp.int32),
        table=pltpu.SMEM((1, phases), F32),
        gm=vm((2 * face, 2 * face), BF16),
        gt=vm((2 * face, 2 * face), BF16),
        sm=vm((2 * face, 2 * face), BF16),
        km=vm((subs * prim, subs * prim), F32),
        pt=vm((face, 4 * prim), BF16),
        coef=vm((face, LANES), F32),
        rc=vm((blocks, prim, LANES), F32),
        rcin=vm((subs, prim, LANES), F32),
        hout=vm((subs, prim, LANES), F32),
        hin=vm((blocks, prim, LANES), F32),
        gin=vm((groups, blocks, prim, LANES), F32),
        e3=vm((n, 4 * prim, chunk), BF16),
        alpha=vm((n * per, 1, LANES), F32),
        ra=vm((span * groups, 1, LANES), F32),
        rbt=vm((rows_b, 1, LANES), F32),
        a1=vm((groups, span, 1, LANES), F32),
        a2=vm((xs, span, 1, LANES), F32),
        a3=vm((zs, span, 1, LANES), F32),
        a4=vm((groups, span, 1, LANES), F32),
        a2o=vm((span, 1, LANES), F32),
        a3o=vm((span, 1, LANES), F32),
        a4o=vm((span, 1, LANES), F32),
        b1=vm((groups, rows_b, 1, LANES), F32),
        b2=vm((subs, rows_b, 1, LANES), F32),
        b2o=vm((rows_b, 1, LANES), F32),
        rs_sem=dma((n,)),
        mat_sem=dma((6,)),
        rc_ss=dma((blocks,)),
        rc_rs=dma(()),
        h_ss=dma((subs,)),
        h_rs=dma(()),
        g_ss=dma((groups,)),
        g_rs=dma(()),
    )
    for name in ("rb", "v", "zb", "y"):
        out[name + "_ss"] = dma((n,))
        out[name + "_rs"] = dma((n,))
    for name, count in (("a1", groups), ("a2", xs), ("a3", zs), ("a4", groups), ("b1", groups), ("b2", subs)):
        out[name + "_ss"] = dma((count,))
        out[name + "_rs"] = dma(())
    return out


def solution(mesh, chunk=CHUNK):
    def body(right_side, schur, inv_factor, coarse_inverse, primal_index, phase, phase_coef):
        face, width = right_side.shape
        cfg = plan(mesh, width, chunk)
        shapes = scratch(cfg, face, primal_index.shape[1], phase_coef.shape[0])
        keys = list(shapes)

        def wrapped(*refs):
            kernel(cfg, *refs[:9], dict(zip(keys, refs[9:])))

        hbm = pl.BlockSpec(memory_space=pltpu.HBM)
        vmem = pl.BlockSpec(memory_space=pltpu.VMEM)
        out = jax.ShapeDtypeStruct((face, width), F32)
        operands = (right_side, schur, inv_factor, coarse_inverse, primal_index)
        operands += (phase.reshape(1, face), phase_coef.reshape(1, -1))
        return pl.pallas_call(
            wrapped,
            out_shape=(out, out),
            in_specs=[hbm] * 7,
            out_specs=(vmem, vmem),
            scratch_shapes=[shapes[k] for k in keys],
            compiler_params=pltpu.CompilerParams(
                collective_id=0, has_side_effects=True, vmem_limit_bytes=44 * 1024 * 1024
            ),
            name="bddc_step",
        )(*[pltpu.with_memory_space_constraint(a, pltpu.HBM) for a in operands])

    both = ("grp", "sub")
    in_specs = (
        P(both, None),
        P(both, None),
        P(both, None),
        P("grp", None),
        P(both, None),
        P(both),
        P(),
    )
    out_specs = (P(both, None), P(both, None))
    return jax.shard_map(body, mesh=mesh, in_specs=in_specs, out_specs=out_specs, check_vma=False)
```

```python
import functools

import jax
import jax.numpy as jnp
from jax import lax
from jax.experimental import pallas as pl
from jax.experimental.pallas import tpu as pltpu
from jax.sharding import PartitionSpec as P

MESH = pl.DeviceIdType.MESH
F32 = jnp.float32
BF16 = jnp.bfloat16
CHUNK = 256
LANES = 128
LATE = 3
HOLD = 1
HEAD = 0
LEAD = 0
AHEAD = 2
ORDER = "wrmwrmSwHrmwrmWwrmwrmVwmCDDDwm"


def plan(mesh, width, chunk):
    groups, subs = mesh.shape["grp"], mesh.shape["sub"]
    depth = 8 if subs >= 16 else 4
    chunks = width // chunk
    return dict(
        groups=groups,
        subs=subs,
        zs=depth,
        xs=subs // depth,
        chunk=chunk,
        chunks=chunks,
        per=chunk // LANES,
        blocks=width // LANES,
        order=ORDER,
        lead=LEAD,
        stride=max(1, subs // (width // LANES)),
        late=LATE,
        head=HEAD,
    )


def kernel(cfg, rs_hbm, s_hbm, g_hbm, k_hbm, idx_hbm, phase_hbm, table_hbm, sol_ref, res_ref, sc):
    groups, subs, zs, xs = cfg["groups"], cfg["subs"], cfg["zs"], cfg["xs"]
    chunk, chunks, per = cfg["chunk"], cfg["chunks"], cfg["per"]
    blocks, stride, late = cfg["blocks"], cfg["stride"], cfg["late"]
    early = chunks - late
    head = cfg["head"]
    face = rs_hbm.shape[0]
    prim = idx_hbm.shape[1]
    idx_ref, phase_ref, table_ref = sc["idx"], sc["phase"], sc["table"]
    g = lax.axis_index("grp")
    j = lax.axis_index("sub")
    x, z = j // zs, lax.rem(j, zs)
    right = lax.rem(j + 1, subs)
    left = lax.rem(j + subs - 1, subs)
    low = pl.ds(face, face)
    up = pl.ds(0, face)

    def remote(src, dst, ssem, rsem, where):
        return pltpu.make_async_remote_copy(
            src_ref=src, dst_ref=dst, send_sem=ssem, recv_sem=rsem, device_id=where, device_id_type=MESH
        )

    def drain(ref, sem):
        pltpu.make_async_copy(ref, ref, sem).wait()

    def cols(c):
        return pl.ds(pl.multiple_of(c * chunk, chunk), chunk)

    def load_rs(c):
        return pltpu.make_async_copy(rs_hbm.at[:, cols(c)], sc["rs"].at[c], sc["rs_sem"].at[c])

    load_g = pltpu.make_async_copy(g_hbm, sc["gm"], sc["mat_sem"].at[0])
    load_k = pltpu.make_async_copy(k_hbm, sc["km"], sc["mat_sem"].at[1])
    load_s = pltpu.make_async_copy(s_hbm, sc["sm"], sc["mat_sem"].at[2])

    def rb_copy(c):
        return remote(
            sc["ext"].at[c, low], sc["ext"].at[c, up], sc["rb_ss"].at[c], sc["rb_rs"].at[c], {"sub": right}
        )

    def v_copy(c):
        return remote(sc["v"].at[c, up], sc["vr"].at[c], sc["v_ss"].at[c], sc["v_rs"].at[c], {"sub": left})

    def zb_copy(c):
        return remote(
            sc["dir"].at[c, low], sc["dir"].at[c, up], sc["zb_ss"].at[c], sc["zb_rs"].at[c], {"sub": right}
        )

    def y_copy(c):
        return remote(sc["y"].at[c, up], sc["yr"].at[c], sc["y_ss"].at[c], sc["y_rs"].at[c], {"sub": left})

    small = [
        pltpu.make_async_copy(idx_hbm, idx_ref, sc["mat_sem"].at[3]),
        pltpu.make_async_copy(phase_hbm, phase_ref, sc["mat_sem"].at[4]),
        pltpu.make_async_copy(table_hbm, table_ref, sc["mat_sem"].at[5]),
    ]

    for c in range(chunks):
        load_rs(c).start()
    for load in small:
        load.start()
    load_g.start()
    load_k.start()
    load_s.start()
    barrier = pltpu.get_barrier_semaphore()

    def greet(sem, where):
        pl.semaphore_signal(sem, inc=1, device_id=where, device_id_type=MESH)

    def greet_grp(d, carry):
        greet(barrier, {"grp": lax.rem(g + d, groups)})
        return carry

    def greet_sub(d, carry):
        greet(barrier, {"sub": lax.rem(j + d, subs)})
        return carry

    lax.fori_loop(1, subs, greet_sub, 0)
    lax.fori_loop(1, groups, greet_grp, 0)

    def cast(c):
        load_rs(c).wait()
        sc["ext"][c, low, :] = sc["rs"][c].astype(BF16)

    def cast_all(c, carry):
        cast(c)
        return carry

    lax.fori_loop(0, chunks, cast_all, 0)

    def pick(c, carry):
        for k in range(prim):
            row = sc["rs"][c, pl.ds(idx_ref[0, k], 1), :]
            for h in range(per):
                sc["rc"][c * per + h, k : k + 1, :] = row[:, h * LANES : (h + 1) * LANES]
        return carry

    for load in small:
        load.wait()
    lax.fori_loop(0, chunks, pick, 0)

    def rc_copy(b):
        return remote(
            sc["rc"].at[b], sc["rcin"].at[j], sc["rc_ss"].at[b], sc["rc_rs"], {"sub": b * stride}
        )

    def rc_send(b, carry):
        @pl.when(b * stride != j)
        def _():
            rc_copy(b).start()

        @pl.when(b * stride == j)
        def _():
            sc["rcin"][j] = sc["rc"][b]

        return carry

    pl.semaphore_wait(barrier, groups - 1 + subs - 1)
    lax.fori_loop(0, blocks, rc_send, 0)
    for c in range(AHEAD):
        rb_copy(c).start()

    load_g.wait()
    sc["gt"][...] = sc["gm"][...].T
    lane = lax.broadcasted_iota(jnp.int32, (4 * prim, face), 1)
    sub_i = lax.broadcasted_iota(jnp.int32, (4 * prim, face), 0)
    which = jnp.full((4 * prim, face), -1, jnp.int32)
    for k in range(prim):
        which = jnp.where(lax.rem(sub_i, prim) == k, idx_ref[0, k], which)
    hot = jnp.where((lane == which) & (sub_i < 3 * prim), 1.0, 0.0).astype(F32)
    sc["pt"][...] = hot.T.astype(BF16)
    labels = phase_ref[...]
    coef = jnp.zeros(labels.shape, F32)
    for k in range(table_ref.shape[1]):
        coef = jnp.where(labels == k, table_ref[0, k], coef)
    sc["coef"][...] = jnp.broadcast_to(coef, (LANES, face)).T
    sc["ra"][...] = jnp.zeros_like(sc["ra"])

    pt_copy = remote(sc["pt"], sc["ptl"], sc["el_ss"].at[0], sc["el_rs"].at[0], {"sub": right})
    el_copy = remote(sc["el"], sc["ell"], sc["el_ss"].at[1], sc["el_rs"].at[1], {"sub": right})
    if head:
        pt_copy.start()
    def first(c):
        u = jnp.dot(sc["gm"][...], sc["ext"][c], preferred_element_type=F32).astype(BF16)
        sc["v"][c] = jnp.dot(sc["gt"][...], u, preferred_element_type=F32).astype(BF16)
        v_copy(c).start()

    is_solver = (lax.rem(j, stride) == 0) & (j < blocks * stride)
    my_block = j // stride

    def h_copy(t):
        return remote(
            sc["hout"].at[t], sc["hin"].at[my_block], sc["h_ss"].at[t], sc["h_rs"], {"sub": t}
        )

    def solve():
        @pl.when(is_solver)
        def _():
            load_k.wait()
            drain(sc["rcin"].at[pl.ds(0, subs - 1)], sc["rc_rs"])
            rhs = sc["rcin"][...].reshape(subs * prim, LANES)
            h = jnp.dot(sc["km"][...], rhs, precision=lax.Precision.HIGHEST, preferred_element_type=F32)
            sc["hout"][...] = h.reshape(subs, prim, LANES)

        @pl.when(jnp.logical_not(is_solver))
        def _():
            load_k.wait()

    def give():
        @pl.when(is_solver)
        def _():
            def h_send(d, carry):
                h_copy(lax.rem(j + d, subs)).start()
                return carry

            lax.fori_loop(1, subs, h_send, 0)
            sc["hin"][my_block] = sc["hout"][j]

    cores = 2
    ys = groups // cores
    row, core = g // cores, lax.rem(g, cores)

    def g_copy(t):
        return remote(sc["hin"], sc["gin"].at[row], sc["g_ss"].at[t], sc["g_rs"], {"grp": t * cores + core})

    pair_copy = remote(
        sc["ysum"], sc["yother"], sc["p_ss"], sc["p_rs"], {"grp": row * cores + 1 - core}
    )

    def share():
        @pl.when(is_solver)
        def _():
            drain(sc["hin"].at[pl.ds(0, blocks - 1)], sc["h_rs"])

        @pl.when(jnp.logical_not(is_solver))
        def _():
            drain(sc["hin"], sc["h_rs"])

        for d in range(1, ys):
            g_copy(lax.rem(row + d, ys)).start()
        sc["gin"][row] = sc["hin"][...]

    def pair():
        if ys > 1:
            drain(sc["gin"].at[pl.ds(0, ys - 1)], sc["g_rs"])
        total = sc["gin"][0]
        for t in range(1, ys):
            total = total + sc["gin"][t]
        sc["ysum"][...] = total
        pair_copy.start()

    def split(e):
        hi = e.astype(BF16).astype(F32)
        rest = e - hi
        mid = rest.astype(BF16).astype(F32)
        tail = rest - mid
        return jnp.concatenate([hi, mid, tail, jnp.zeros_like(hi)], axis=0).astype(BF16)

    def correct():
        pair_copy.wait_recv()
        for b in range(blocks):
            total = sc["ysum"][b] + sc["yother"][b]
            e = sc["hin"][b] + total / groups
            c, h = divmod(b, per)
            sc["e3"][c, :, h * LANES : (h + 1) * LANES] = split(e)
            if c < head:
                sc["el"][b] = e
        if head:
            el_copy.start()

    def rows_to(ref, base, c, value):
        for h in range(per):
            ref[base + c * per + h] = value[:, h * LANES : (h + 1) * LANES]

    def low_copy(c):
        return remote(
            sc["v"].at[c, low], sc["dir"].at[c, up], sc["zb_ss"].at[c], sc["zb_rs"].at[c], {"sub": right}
        )

    def left_direction(c):
        stack = [split(sc["ell"][c * per + h]) for h in range(per)]
        fix = jnp.dot(sc["ptl"][...], jnp.concatenate(stack, axis=1), preferred_element_type=F32)
        both = sc["dir"][c, up, :].astype(F32) + sc["v"][c, up, :].astype(F32)
        sc["dir"][c, up, :] = (0.5 * both + fix).astype(BF16)

    def direction(c, send=True):
        v_copy(c).wait_recv()
        fix = jnp.dot(sc["pt"][...], sc["e3"][c], preferred_element_type=F32)
        both = sc["v"][c, low, :].astype(F32) + sc["vr"][c].astype(F32)
        zz = 0.5 * both + fix
        sc["dir"][c, low, :] = zz.astype(BF16)
        if send:
            zb_copy(c).start()
        rows_to(sc["ra"], 0, c, jnp.sum(sc["rs"][c] * zz, axis=0, keepdims=True))

    def wide_coef():
        return jnp.concatenate([sc["coef"][...]] * per, axis=1)

    def image(c, ref, base, send=True):
        y = jnp.dot(sc["sm"][...], sc["dir"][c], preferred_element_type=F32).astype(BF16)
        sc["y"][c] = y
        if send:
            y_copy(c).start()
        zf = sc["dir"][c, low, :].astype(F32)
        part = jnp.sum(sc["dir"][c].astype(F32) * sc["y"][c].astype(F32), axis=0, keepdims=True)
        part = part + jnp.sum(wide_coef() * zf * zf, axis=0, keepdims=True)
        rows_to(ref, base, c, part)

    def finish(c, carry):
        y_copy(c).wait_recv()
        alpha = jnp.concatenate([sc["alpha"][c * per + h] for h in range(per)], axis=1)
        zf = sc["dir"][c, low, :].astype(F32)
        q = sc["y"][c, low, :].astype(F32) + sc["yr"][c].astype(F32) + wide_coef() * zf
        sol_ref[:, cols(c)] = alpha * zf
        res_ref[:, cols(c)] = sc["rs"][c] - alpha * q
        return carry

    span = sc["ra"].shape[0] // groups

    def exchange(name, count, me, where, src_of):
        def copy(t):
            return remote(src_of(t), sc[name].at[me], sc[name + "_ss"].at[t], sc[name + "_rs"], where(t))

        def start(own):
            def go(d, carry):
                copy(lax.rem(me + d, count)).start()
                return carry

            lax.fori_loop(1, count, go, 0)
            sc[name][me] = own

        def end():
            drain(sc[name].at[pl.ds(0, count - 1)], sc[name + "_rs"])
            total = sc[name][0]
            for t in range(1, count):
                total = total + sc[name][t]
            return total

        def sent():
            def go(d, carry):
                copy(lax.rem(me + d, count)).wait_send()
                return carry

            lax.fori_loop(1, count, go, 0)

        return start, end, sent

    to_grp = lambda t: {"grp": t}
    to_x = lambda t: {"sub": t * zs + z}
    to_z = lambda t: {"sub": x * zs + t}
    a1 = exchange("a1", groups, g, to_grp, lambda t: sc["ra"].at[pl.ds(t * span, span)])
    a2 = exchange("a2", xs, x, to_x, lambda t: sc["a2o"])
    a3 = exchange("a3", zs, z, to_z, lambda t: sc["a3o"])
    a4 = exchange("a4", groups, g, to_grp, lambda t: sc["a4o"])
    b1 = exchange("b1", groups, g, to_grp, lambda t: sc["rbt"])
    b2 = exchange("b2", subs, j, lambda t: {"sub": t}, lambda t: sc["b2o"])

    def hop(before, after, name):
        total = before[1]()
        sc[name][...] = total
        after[0](total)

    count = {"w": 0, "m": 0, "r": AHEAD, "L": 0, "D": 0}
    actions = {
        "w": lambda c: rb_copy(c).wait_recv(),
        "m": first,
        "r": lambda c: rb_copy(c).start(),
        "L": lambda c: low_copy(c).start(),
        "D": lambda c: direction(c, send=c >= head),
    }
    steps = {"S": solve, "H": give, "W": share, "V": pair, "C": correct}
    lead = cfg["lead"]
    for step in cfg["order"]:
        if step in steps:
            steps[step]()
        else:
            actions[step](count[step])
            count[step] += 1
    load_s.wait()
    base = chunks * per

    ready = max(head, count["D"])
    for c in range(ready, min(chunks, ready + lead)):
        direction(c)
    ready = min(chunks, ready + lead)
    if head:
        pt_copy.wait_recv()
        el_copy.wait_recv()
    for c in range(chunks):
        if c == early:
            a1[0](sc["ra"][pl.ds(g * span, span)])
        if c == early + 1:
            hop(a1, a2, "a2o")
        if c == early + 2:
            hop(a2, a3, "a3o")
        if c < head and c >= count["D"]:
            direction(c, send=False)
        if ready < chunks and c >= head:
            direction(ready)
            ready += 1
        zb_copy(c).wait_recv()
        if c < head:
            left_direction(c)
        if ready < chunks and c < head:
            direction(ready)
            ready += 1
        if c < early:
            image(c, sc["ra"], base)
        else:
            image(c, sc["rbt"], -early * per, send=c < chunks - HOLD)
    b1[0](sc["rbt"][...])
    if late < 3:
        hop(a2, a3, "a3o")
    hop(b1, b2, "b2o")
    for c in range(chunks - HOLD, chunks):
        y_copy(c).start()
    hop(a3, a4, "a4o")
    drain(sc["a4"].at[pl.ds(0, groups - 1)], sc["a4_rs"])
    for r in range(early * per):
        n, d = r, base + r
        sc["alpha"][r] = sc["a4"][n // span, n % span] / sc["a4"][d // span, d % span]
    lax.fori_loop(0, early, finish, 0)
    last = b2[1]()
    for r in range(late * per):
        n = early * per + r
        sc["alpha"][n] = sc["a4"][n // span, n % span] / last[r]
    lax.fori_loop(early, chunks, finish, 0)

    if head:
        pt_copy.wait_send()
        el_copy.wait_send()

    def drain_streams(c, carry):
        rb_copy(c).wait_send()
        v_copy(c).wait_send()
        zb_copy(c).wait_send()
        y_copy(c).wait_send()
        return carry

    lax.fori_loop(0, chunks, drain_streams, 0)

    def drain_rc(b, carry):
        @pl.when(b * stride != j)
        def _():
            rc_copy(b).wait_send()

        return carry

    lax.fori_loop(0, blocks, drain_rc, 0)

    @pl.when(is_solver)
    def _():
        def drain_h(d, carry):
            h_copy(lax.rem(j + d, subs)).wait_send()
            return carry

        lax.fori_loop(1, subs, drain_h, 0)

    for d in range(1, ys):
        g_copy(lax.rem(row + d, ys)).wait_send()
    pair_copy.wait_send()
    for stage in (a1, a2, a3, a4, b1, b2):
        stage[2]()


def write_out(sol_ref, res_ref, sol_hbm, res_hbm, sems):
    copies = [
        pltpu.make_async_copy(sol_ref, sol_hbm, sems.at[0]),
        pltpu.make_async_copy(res_ref, res_hbm, sems.at[1]),
    ]
    for copy in copies:
        copy.start()
    for copy in copies:
        copy.wait()


def scratch(cfg, face, prim, phases):
    n, chunk, per = cfg["chunks"], cfg["chunk"], cfg["per"]
    groups, subs, xs, zs, blocks = cfg["groups"], cfg["subs"], cfg["xs"], cfg["zs"], cfg["blocks"]
    rows_a = (2 * n - cfg["late"]) * per
    span = -(-rows_a // groups)
    rows_b = cfg["late"] * per
    vm, dma = pltpu.VMEM, pltpu.SemaphoreType.DMA
    out = dict(
        rs=vm((n, face, chunk), F32),
        ext=vm((n, 2 * face, chunk), BF16),
        v=vm((n, 2 * face, chunk), BF16),
        vr=vm((n, face, chunk), BF16),
        dir=vm((n, 2 * face, chunk), BF16),
        y=vm((n, 2 * face, chunk), BF16),
        yr=vm((n, face, chunk), BF16),
        ptl=vm((face, 4 * prim), BF16),
        el=vm((max(cfg["head"], 1) * per, prim, LANES), F32),
        ell=vm((max(cfg["head"], 1) * per, prim, LANES), F32),
        el_ss=dma((2,)),
        el_rs=dma((2,)),
        idx=pltpu.SMEM((1, prim), jnp.int32),
        phase=vm((1, face), jnp.int32),
        table=pltpu.SMEM((1, phases), F32),
        gm=vm((2 * face, 2 * face), BF16),
        gt=vm((2 * face, 2 * face), BF16),
        sm=vm((2 * face, 2 * face), BF16),
        km=vm((subs * prim, subs * prim), F32),
        pt=vm((face, 4 * prim), BF16),
        coef=vm((face, LANES), F32),
        rc=vm((blocks, prim, LANES), F32),
        rcin=vm((subs, prim, LANES), F32),
        hout=vm((subs, prim, LANES), F32),
        hin=vm((blocks, prim, LANES), F32),
        gin=vm((groups // 2, blocks, prim, LANES), F32),
        ysum=vm((blocks, prim, LANES), F32),
        yother=vm((blocks, prim, LANES), F32),
        e3=vm((n, 4 * prim, chunk), BF16),
        alpha=vm((n * per, 1, LANES), F32),
        ra=vm((span * groups, 1, LANES), F32),
        rbt=vm((rows_b, 1, LANES), F32),
        a1=vm((groups, span, 1, LANES), F32),
        a2=vm((xs, span, 1, LANES), F32),
        a3=vm((zs, span, 1, LANES), F32),
        a4=vm((groups, span, 1, LANES), F32),
        a2o=vm((span, 1, LANES), F32),
        a3o=vm((span, 1, LANES), F32),
        a4o=vm((span, 1, LANES), F32),
        b1=vm((groups, rows_b, 1, LANES), F32),
        b2=vm((subs, rows_b, 1, LANES), F32),
        b2o=vm((rows_b, 1, LANES), F32),
        rs_sem=dma((n,)),
        mat_sem=dma((6,)),
        rc_ss=dma((blocks,)),
        rc_rs=dma(()),
        h_ss=dma((subs,)),
        h_rs=dma(()),
        g_ss=dma((groups // 2,)),
        p_ss=dma(()),
        p_rs=dma(()),
        g_rs=dma(()),
    )
    for name in ("rb", "v", "zb", "y"):
        out[name + "_ss"] = dma((n,))
        out[name + "_rs"] = dma((n,))
    for name, count in (("a1", groups), ("a2", xs), ("a3", zs), ("a4", groups), ("b1", groups), ("b2", subs)):
        out[name + "_ss"] = dma((count,))
        out[name + "_rs"] = dma(())
    return out


def solution(mesh, chunk=CHUNK):
    def body(right_side, schur, inv_factor, coarse_inverse, primal_index, phase, phase_coef):
        face, width = right_side.shape
        cfg = plan(mesh, width, chunk)
        shapes = scratch(cfg, face, primal_index.shape[1], phase_coef.shape[0])
        keys = list(shapes)

        def wrapped(*refs):
            kernel(cfg, *refs[:9], dict(zip(keys, refs[9:])))

        hbm = pl.BlockSpec(memory_space=pltpu.HBM)
        vmem = pl.BlockSpec(memory_space=pltpu.VMEM)
        out = jax.ShapeDtypeStruct((face, width), F32)
        operands = (right_side, schur, inv_factor, coarse_inverse, primal_index)
        operands += (phase.reshape(1, face), phase_coef.reshape(1, -1))
        held = pltpu.VMEM((face, width), F32)
        results = pl.pallas_call(
            wrapped,
            out_shape=(held, held),
            in_specs=[hbm] * 7,
            out_specs=(vmem, vmem),
            scratch_shapes=[shapes[k] for k in keys],
            compiler_params=pltpu.CompilerParams(
                collective_id=0, has_side_effects=True, vmem_limit_bytes=44 * 1024 * 1024
            ),
            name="bddc_step",
        )(*[pltpu.with_memory_space_constraint(a, pltpu.HBM) for a in operands])
        return pl.pallas_call(
            write_out,
            out_shape=(out, out),
            in_specs=[vmem, vmem],
            out_specs=(hbm, hbm),
            scratch_shapes=[pltpu.SemaphoreType.DMA((2,))],
            compiler_params=pltpu.CompilerParams(vmem_limit_bytes=1024 * 1024),
            name="write_out",
        )(*results)

    both = ("grp", "sub")
    in_specs = (
        P(both, None),
        P(both, None),
        P(both, None),
        P("grp", None),
        P(both, None),
        P(both),
        P(),
    )
    out_specs = (P(both, None), P(both, None))
    return jax.shard_map(body, mesh=mesh, in_specs=in_specs, out_specs=out_specs, check_vma=False)
```

```python
import functools

import jax
import jax.numpy as jnp
from jax import lax
from jax.experimental import pallas as pl
from jax.experimental.pallas import tpu as pltpu
from jax.sharding import PartitionSpec as P

MESH = pl.DeviceIdType.MESH
F32 = jnp.float32
BF16 = jnp.bfloat16
CHUNK = 256
LANES = 128
LATE = 3
HOLD = 0
HEAD = 0
LEAD = 0
AHEAD = 2
ORDER = "wrmwSHrmwrmwrmWwrmVwrmCDDwmDwm"


def plan(mesh, width, chunk):
    groups, subs = mesh.shape["grp"], mesh.shape["sub"]
    depth = 8 if subs >= 16 else 4
    chunks = width // chunk
    return dict(
        groups=groups,
        subs=subs,
        zs=depth,
        xs=subs // depth,
        chunk=chunk,
        chunks=chunks,
        per=chunk // LANES,
        blocks=width // LANES,
        order=ORDER,
        lead=LEAD,
        stride=max(1, subs // (width // LANES)),
        late=LATE,
        head=HEAD,
    )


def kernel(cfg, rs_hbm, s_hbm, g_hbm, k_hbm, idx_hbm, phase_hbm, table_hbm, sol_ref, res_ref, sc):
    groups, subs, zs, xs = cfg["groups"], cfg["subs"], cfg["zs"], cfg["xs"]
    chunk, chunks, per = cfg["chunk"], cfg["chunks"], cfg["per"]
    blocks, stride, late = cfg["blocks"], cfg["stride"], cfg["late"]
    early = chunks - late
    head = cfg["head"]
    face = rs_hbm.shape[0]
    prim = idx_hbm.shape[1]
    idx_ref, phase_ref, table_ref = sc["idx"], sc["phase"], sc["table"]
    g = lax.axis_index("grp")
    j = lax.axis_index("sub")
    x, z = j // zs, lax.rem(j, zs)
    right = lax.rem(j + 1, subs)
    left = lax.rem(j + subs - 1, subs)
    low = pl.ds(face, face)
    up = pl.ds(0, face)

    def remote(src, dst, ssem, rsem, where):
        return pltpu.make_async_remote_copy(
            src_ref=src, dst_ref=dst, send_sem=ssem, recv_sem=rsem, device_id=where, device_id_type=MESH
        )

    def drain(ref, sem):
        pltpu.make_async_copy(ref, ref, sem).wait()

    def cols(c):
        return pl.ds(pl.multiple_of(c * chunk, chunk), chunk)

    def load_rs(c):
        return pltpu.make_async_copy(rs_hbm.at[:, cols(c)], sc["rs"].at[c], sc["rs_sem"].at[c])

    load_g = pltpu.make_async_copy(g_hbm, sc["gm"], sc["mat_sem"].at[0])
    load_k = pltpu.make_async_copy(k_hbm, sc["km"], sc["mat_sem"].at[1])
    load_s = pltpu.make_async_copy(s_hbm, sc["sm"], sc["mat_sem"].at[2])

    def rb_copy(c):
        return remote(
            sc["ext"].at[c, low], sc["ext"].at[c, up], sc["rb_ss"].at[c], sc["rb_rs"].at[c], {"sub": right}
        )

    def v_copy(c):
        return remote(sc["v"].at[c, up], sc["vr"].at[c], sc["v_ss"].at[c], sc["v_rs"].at[c], {"sub": left})

    def zb_copy(c):
        return remote(
            sc["dir"].at[c, low], sc["dir"].at[c, up], sc["zb_ss"].at[c], sc["zb_rs"].at[c], {"sub": right}
        )

    def y_copy(c):
        return remote(sc["y"].at[c, up], sc["yr"].at[c], sc["y_ss"].at[c], sc["y_rs"].at[c], {"sub": left})

    small = [
        pltpu.make_async_copy(idx_hbm, idx_ref, sc["mat_sem"].at[3]),
        pltpu.make_async_copy(phase_hbm, phase_ref, sc["mat_sem"].at[4]),
        pltpu.make_async_copy(table_hbm, table_ref, sc["mat_sem"].at[5]),
    ]

    barrier = pltpu.get_barrier_semaphore()

    def greet(sem, where):
        pl.semaphore_signal(sem, inc=1, device_id=where, device_id_type=MESH)

    def greet_grp(d, carry):
        greet(barrier, {"grp": lax.rem(g + d, groups)})
        return carry

    def greet_sub(d, carry):
        greet(barrier, {"sub": lax.rem(j + 1 + lax.rem(d + subs // 3, subs - 1), subs)})
        return carry

    lax.fori_loop(1, subs, greet_sub, 0)
    lax.fori_loop(1, groups, greet_grp, 0)
    for c in range(chunks):
        load_rs(c).start()
    for load in small:
        load.start()
    load_g.start()
    load_k.start()
    load_s.start()

    def cast(c):
        load_rs(c).wait()
        sc["ext"][c, low, :] = sc["rs"][c].astype(BF16)

    def cast_all(c, carry):
        cast(c)
        return carry

    lax.fori_loop(0, chunks, cast_all, 0)

    def pick(c, carry):
        for k in range(prim):
            row = sc["rs"][c, pl.ds(idx_ref[0, k], 1), :]
            for h in range(per):
                sc["rc"][c * per + h, k : k + 1, :] = row[:, h * LANES : (h + 1) * LANES]
        return carry

    for load in small:
        load.wait()
    lax.fori_loop(0, chunks, pick, 0)

    def rc_copy(b):
        return remote(
            sc["rc"].at[b], sc["rcin"].at[j], sc["rc_ss"].at[b], sc["rc_rs"], {"sub": b * stride}
        )

    def rc_send(b, carry):
        @pl.when(b * stride != j)
        def _():
            rc_copy(b).start()

        @pl.when(b * stride == j)
        def _():
            sc["rcin"][j] = sc["rc"][b]

        return carry

    load_g.wait()
    sc["gt"][...] = sc["gm"][...].T
    lane = lax.broadcasted_iota(jnp.int32, (4 * prim, face), 1)
    sub_i = lax.broadcasted_iota(jnp.int32, (4 * prim, face), 0)
    which = jnp.full((4 * prim, face), -1, jnp.int32)
    for k in range(prim):
        which = jnp.where(lax.rem(sub_i, prim) == k, idx_ref[0, k], which)
    hot = jnp.where((lane == which) & (sub_i < 3 * prim), 1.0, 0.0).astype(F32)
    sc["pt"][...] = hot.T.astype(BF16)
    labels = phase_ref[...]
    coef = jnp.zeros(labels.shape, F32)
    for k in range(table_ref.shape[1]):
        coef = jnp.where(labels == k, table_ref[0, k], coef)
    sc["coef"][...] = jnp.broadcast_to(coef, (LANES, face)).T
    sc["ra"][...] = jnp.zeros_like(sc["ra"])

    pl.semaphore_wait(barrier, groups - 1 + subs - 1)
    lax.fori_loop(0, blocks, rc_send, 0)
    for c in range(AHEAD):
        rb_copy(c).start()

    pt_copy = remote(sc["pt"], sc["ptl"], sc["el_ss"].at[0], sc["el_rs"].at[0], {"sub": right})
    el_copy = remote(sc["el"], sc["ell"], sc["el_ss"].at[1], sc["el_rs"].at[1], {"sub": right})
    if head:
        pt_copy.start()
    def first(c):
        u = jnp.dot(sc["gm"][...], sc["ext"][c], preferred_element_type=F32).astype(BF16)
        sc["v"][c] = jnp.dot(sc["gt"][...], u, preferred_element_type=F32).astype(BF16)
        v_copy(c).start()

    is_solver = (lax.rem(j, stride) == 0) & (j < blocks * stride)
    my_block = j // stride

    def h_copy(t):
        return remote(
            sc["hout"].at[t], sc["hin"].at[my_block], sc["h_ss"].at[t], sc["h_rs"], {"sub": t}
        )

    def solve():
        @pl.when(is_solver)
        def _():
            load_k.wait()
            drain(sc["rcin"].at[pl.ds(0, subs - 1)], sc["rc_rs"])
            rhs = sc["rcin"][...].reshape(subs * prim, LANES)
            h = jnp.dot(sc["km"][...], rhs, precision=lax.Precision.HIGHEST, preferred_element_type=F32)
            sc["hout"][...] = h.reshape(subs, prim, LANES)

        @pl.when(jnp.logical_not(is_solver))
        def _():
            load_k.wait()

    def give():
        @pl.when(is_solver)
        def _():
            def h_send(d, carry):
                h_copy(lax.rem(j + d, subs)).start()
                return carry

            lax.fori_loop(1, subs, h_send, 0)
            sc["hin"][my_block] = sc["hout"][j]

    cores = 2
    ys = groups // cores
    row, core = g // cores, lax.rem(g, cores)

    def g_copy(t):
        return remote(sc["hin"], sc["gin"].at[row], sc["g_ss"].at[t], sc["g_rs"], {"grp": t * cores + core})

    pair_copy = remote(
        sc["ysum"], sc["yother"], sc["p_ss"], sc["p_rs"], {"grp": row * cores + 1 - core}
    )

    def share():
        @pl.when(is_solver)
        def _():
            drain(sc["hin"].at[pl.ds(0, blocks - 1)], sc["h_rs"])

        @pl.when(jnp.logical_not(is_solver))
        def _():
            drain(sc["hin"], sc["h_rs"])

        for d in range(1, ys):
            g_copy(lax.rem(row + d, ys)).start()
        sc["gin"][row] = sc["hin"][...]

    def pair():
        if ys > 1:
            drain(sc["gin"].at[pl.ds(0, ys - 1)], sc["g_rs"])
        total = sc["gin"][0]
        for t in range(1, ys):
            total = total + sc["gin"][t]
        sc["ysum"][...] = total
        pair_copy.start()

    def split(e):
        hi = e.astype(BF16).astype(F32)
        rest = e - hi
        mid = rest.astype(BF16).astype(F32)
        tail = rest - mid
        return jnp.concatenate([hi, mid, tail, jnp.zeros_like(hi)], axis=0).astype(BF16)

    def correct():
        pair_copy.wait_recv()
        for b in range(blocks):
            total = sc["ysum"][b] + sc["yother"][b]
            e = sc["hin"][b] + total / groups
            c, h = divmod(b, per)
            sc["e3"][c, :, h * LANES : (h + 1) * LANES] = split(e)
            if c < head:
                sc["el"][b] = e
        if head:
            el_copy.start()

    def rows_to(ref, base, c, value):
        for h in range(per):
            ref[base + c * per + h] = value[:, h * LANES : (h + 1) * LANES]

    def low_copy(c):
        return remote(
            sc["v"].at[c, low], sc["dir"].at[c, up], sc["zb_ss"].at[c], sc["zb_rs"].at[c], {"sub": right}
        )

    def left_direction(c):
        stack = [split(sc["ell"][c * per + h]) for h in range(per)]
        fix = jnp.dot(sc["ptl"][...], jnp.concatenate(stack, axis=1), preferred_element_type=F32)
        both = sc["dir"][c, up, :].astype(F32) + sc["v"][c, up, :].astype(F32)
        sc["dir"][c, up, :] = (0.5 * both + fix).astype(BF16)

    def direction(c, send=True):
        v_copy(c).wait_recv()
        fix = jnp.dot(sc["pt"][...], sc["e3"][c], preferred_element_type=F32)
        both = sc["v"][c, low, :].astype(F32) + sc["vr"][c].astype(F32)
        zz = 0.5 * both + fix
        sc["dir"][c, low, :] = zz.astype(BF16)
        if send:
            zb_copy(c).start()
        rows_to(sc["ra"], 0, c, jnp.sum(sc["rs"][c] * zz, axis=0, keepdims=True))

    def wide_coef():
        return jnp.concatenate([sc["coef"][...]] * per, axis=1)

    def image(c, ref, base, send=True):
        y = jnp.dot(sc["sm"][...], sc["dir"][c], preferred_element_type=F32).astype(BF16)
        sc["y"][c] = y
        if send:
            y_copy(c).start()
        zf = sc["dir"][c, low, :].astype(F32)
        part = jnp.sum(sc["dir"][c].astype(F32) * sc["y"][c].astype(F32), axis=0, keepdims=True)
        part = part + jnp.sum(wide_coef() * zf * zf, axis=0, keepdims=True)
        rows_to(ref, base, c, part)

    def finish(c, carry):
        y_copy(c).wait_recv()
        alpha = jnp.concatenate([sc["alpha"][c * per + h] for h in range(per)], axis=1)
        zf = sc["dir"][c, low, :].astype(F32)
        q = sc["y"][c, low, :].astype(F32) + sc["yr"][c].astype(F32) + wide_coef() * zf
        sol_ref[:, cols(c)] = alpha * zf
        res_ref[:, cols(c)] = sc["rs"][c] - alpha * q
        return carry

    span = sc["ra"].shape[0] // groups

    def exchange(name, count, me, where, src_of):
        def copy(t):
            return remote(src_of(t), sc[name].at[me], sc[name + "_ss"].at[t], sc[name + "_rs"], where(t))

        def start(own):
            def go(d, carry):
                copy(lax.rem(me + 1 + lax.rem(d + count // 3, count - 1), count)).start()
                return carry

            lax.fori_loop(1, count, go, 0)
            sc[name][me] = own

        def end():
            drain(sc[name].at[pl.ds(0, count - 1)], sc[name + "_rs"])
            total = sc[name][0]
            for t in range(1, count):
                total = total + sc[name][t]
            return total

        def sent():
            def go(d, carry):
                copy(lax.rem(me + d, count)).wait_send()
                return carry

            lax.fori_loop(1, count, go, 0)

        return start, end, sent

    to_grp = lambda t: {"grp": t}
    to_x = lambda t: {"sub": t * zs + z}
    to_z = lambda t: {"sub": x * zs + t}
    a1 = exchange("a1", groups, g, to_grp, lambda t: sc["ra"].at[pl.ds(t * span, span)])
    a2 = exchange("a2", xs, x, to_x, lambda t: sc["a2o"])
    a3 = exchange("a3", zs, z, to_z, lambda t: sc["a3o"])
    a4 = exchange("a4", groups, g, to_grp, lambda t: sc["a4o"])
    b1 = exchange("b1", groups, g, to_grp, lambda t: sc["rbt"])
    b2 = exchange("b2", subs, j, lambda t: {"sub": t}, lambda t: sc["b2o"])

    def hop(before, after, name):
        total = before[1]()
        sc[name][...] = total
        after[0](total)

    count = {"w": 0, "m": 0, "r": AHEAD, "L": 0, "D": 0}
    actions = {
        "w": lambda c: rb_copy(c).wait_recv(),
        "m": first,
        "r": lambda c: rb_copy(c).start(),
        "L": lambda c: low_copy(c).start(),
        "D": lambda c: direction(c, send=c >= head),
    }
    steps = {"S": solve, "H": give, "W": share, "V": pair, "C": correct}
    lead = cfg["lead"]
    for step in cfg["order"]:
        if step in steps:
            steps[step]()
        else:
            actions[step](count[step])
            count[step] += 1
    load_s.wait()
    base = chunks * per

    ready = max(head, count["D"])
    for c in range(ready, min(chunks, ready + lead)):
        direction(c)
    ready = min(chunks, ready + lead)
    if head:
        pt_copy.wait_recv()
        el_copy.wait_recv()
    for c in range(chunks):
        if c == early:
            a1[0](sc["ra"][pl.ds(g * span, span)])
        if c == early + 1:
            hop(a1, a2, "a2o")
        if c == early + 2:
            hop(a2, a3, "a3o")
        if c < head and c >= count["D"]:
            direction(c, send=False)
        if ready < chunks and c >= head:
            direction(ready)
            ready += 1
        zb_copy(c).wait_recv()
        if c < head:
            left_direction(c)
        if ready < chunks and c < head:
            direction(ready)
            ready += 1
        if c < early:
            image(c, sc["ra"], base)
        else:
            image(c, sc["rbt"], -early * per, send=c < chunks - HOLD)
    b1[0](sc["rbt"][...])
    if late < 3:
        hop(a2, a3, "a3o")
    hop(b1, b2, "b2o")
    for c in range(chunks - HOLD, chunks):
        y_copy(c).start()
    hop(a3, a4, "a4o")
    drain(sc["a4"].at[pl.ds(0, groups - 1)], sc["a4_rs"])
    for r in range(early * per):
        n, d = r, base + r
        sc["alpha"][r] = sc["a4"][n // span, n % span] / sc["a4"][d // span, d % span]
    lax.fori_loop(0, early, finish, 0)
    last = b2[1]()
    for r in range(late * per):
        n = early * per + r
        sc["alpha"][n] = sc["a4"][n // span, n % span] / last[r]
    lax.fori_loop(early, chunks, finish, 0)

    if head:
        pt_copy.wait_send()
        el_copy.wait_send()

    def drain_streams(c, carry):
        rb_copy(c).wait_send()
        v_copy(c).wait_send()
        zb_copy(c).wait_send()
        y_copy(c).wait_send()
        return carry

    lax.fori_loop(0, chunks, drain_streams, 0)

    def drain_rc(b, carry):
        @pl.when(b * stride != j)
        def _():
            rc_copy(b).wait_send()

        return carry

    lax.fori_loop(0, blocks, drain_rc, 0)

    @pl.when(is_solver)
    def _():
        def drain_h(d, carry):
            h_copy(lax.rem(j + d, subs)).wait_send()
            return carry

        lax.fori_loop(1, subs, drain_h, 0)

    for d in range(1, ys):
        g_copy(lax.rem(row + d, ys)).wait_send()
    pair_copy.wait_send()
    for stage in (a1, a2, a3, a4, b1, b2):
        stage[2]()


def write_out(sol_ref, res_ref, sol_hbm, res_hbm, sems):
    copies = [
        pltpu.make_async_copy(sol_ref, sol_hbm, sems.at[0]),
        pltpu.make_async_copy(res_ref, res_hbm, sems.at[1]),
    ]
    for copy in copies:
        copy.start()
    for copy in copies:
        copy.wait()


def scratch(cfg, face, prim, phases):
    n, chunk, per = cfg["chunks"], cfg["chunk"], cfg["per"]
    groups, subs, xs, zs, blocks = cfg["groups"], cfg["subs"], cfg["xs"], cfg["zs"], cfg["blocks"]
    rows_a = (2 * n - cfg["late"]) * per
    span = -(-rows_a // groups)
    rows_b = cfg["late"] * per
    vm, dma = pltpu.VMEM, pltpu.SemaphoreType.DMA
    out = dict(
        rs=vm((n, face, chunk), F32),
        ext=vm((n, 2 * face, chunk), BF16),
        v=vm((n, 2 * face, chunk), BF16),
        vr=vm((n, face, chunk), BF16),
        dir=vm((n, 2 * face, chunk), BF16),
        y=vm((n, 2 * face, chunk), BF16),
        yr=vm((n, face, chunk), BF16),
        ptl=vm((face, 4 * prim), BF16),
        el=vm((max(cfg["head"], 1) * per, prim, LANES), F32),
        ell=vm((max(cfg["head"], 1) * per, prim, LANES), F32),
        el_ss=dma((2,)),
        el_rs=dma((2,)),
        idx=pltpu.SMEM((1, prim), jnp.int32),
        phase=vm((1, face), jnp.int32),
        table=pltpu.SMEM((1, phases), F32),
        gm=vm((2 * face, 2 * face), BF16),
        gt=vm((2 * face, 2 * face), BF16),
        sm=vm((2 * face, 2 * face), BF16),
        km=vm((subs * prim, subs * prim), F32),
        pt=vm((face, 4 * prim), BF16),
        coef=vm((face, LANES), F32),
        rc=vm((blocks, prim, LANES), F32),
        rcin=vm((subs, prim, LANES), F32),
        hout=vm((subs, prim, LANES), F32),
        hin=vm((blocks, prim, LANES), F32),
        gin=vm((groups // 2, blocks, prim, LANES), F32),
        ysum=vm((blocks, prim, LANES), F32),
        yother=vm((blocks, prim, LANES), F32),
        e3=vm((n, 4 * prim, chunk), BF16),
        alpha=vm((n * per, 1, LANES), F32),
        ra=vm((span * groups, 1, LANES), F32),
        rbt=vm((rows_b, 1, LANES), F32),
        a1=vm((groups, span, 1, LANES), F32),
        a2=vm((xs, span, 1, LANES), F32),
        a3=vm((zs, span, 1, LANES), F32),
        a4=vm((groups, span, 1, LANES), F32),
        a2o=vm((span, 1, LANES), F32),
        a3o=vm((span, 1, LANES), F32),
        a4o=vm((span, 1, LANES), F32),
        b1=vm((groups, rows_b, 1, LANES), F32),
        b2=vm((subs, rows_b, 1, LANES), F32),
        b2o=vm((rows_b, 1, LANES), F32),
        rs_sem=dma((n,)),
        mat_sem=dma((6,)),
        rc_ss=dma((blocks,)),
        rc_rs=dma(()),
        h_ss=dma((subs,)),
        h_rs=dma(()),
        g_ss=dma((groups // 2,)),
        p_ss=dma(()),
        p_rs=dma(()),
        g_rs=dma(()),
    )
    for name in ("rb", "v", "zb", "y"):
        out[name + "_ss"] = dma((n,))
        out[name + "_rs"] = dma((n,))
    for name, count in (("a1", groups), ("a2", xs), ("a3", zs), ("a4", groups), ("b1", groups), ("b2", subs)):
        out[name + "_ss"] = dma((count,))
        out[name + "_rs"] = dma(())
    return out


def solution(mesh, chunk=CHUNK):
    def body(right_side, schur, inv_factor, coarse_inverse, primal_index, phase, phase_coef):
        face, width = right_side.shape
        cfg = plan(mesh, width, chunk)
        shapes = scratch(cfg, face, primal_index.shape[1], phase_coef.shape[0])
        keys = list(shapes)

        def wrapped(*refs):
            kernel(cfg, *refs[:9], dict(zip(keys, refs[9:])))

        hbm = pl.BlockSpec(memory_space=pltpu.HBM)
        vmem = pl.BlockSpec(memory_space=pltpu.VMEM)
        out = jax.ShapeDtypeStruct((face, width), F32)
        operands = (right_side, schur, inv_factor, coarse_inverse, primal_index)
        operands += (phase.reshape(1, face), phase_coef.reshape(1, -1))
        held = pltpu.VMEM((face, width), F32)
        results = pl.pallas_call(
            wrapped,
            out_shape=(held, held),
            in_specs=[hbm] * 7,
            out_specs=(vmem, vmem),
            scratch_shapes=[shapes[k] for k in keys],
            compiler_params=pltpu.CompilerParams(
                collective_id=0, has_side_effects=True, vmem_limit_bytes=44 * 1024 * 1024
            ),
            name="bddc_step",
        )(*[pltpu.with_memory_space_constraint(a, pltpu.HBM) for a in operands])
        return pl.pallas_call(
            write_out,
            out_shape=(out, out),
            in_specs=[vmem, vmem],
            out_specs=(hbm, hbm),
            scratch_shapes=[pltpu.SemaphoreType.DMA((2,))],
            compiler_params=pltpu.CompilerParams(vmem_limit_bytes=1024 * 1024),
            name="write_out",
        )(*results)

    both = ("grp", "sub")
    in_specs = (
        P(both, None),
        P(both, None),
        P(both, None),
        P("grp", None),
        P(both, None),
        P(both),
        P(),
    )
    out_specs = (P(both, None), P(both, None))
    return jax.shard_map(body, mesh=mesh, in_specs=in_specs, out_specs=out_specs, check_vma=False)
```

```python
import functools

import jax
import jax.numpy as jnp
from jax import lax
from jax.experimental import pallas as pl
from jax.experimental.pallas import tpu as pltpu
from jax.sharding import PartitionSpec as P

MESH = pl.DeviceIdType.MESH
F32 = jnp.float32
BF16 = jnp.bfloat16
CHUNK = 256
LANES = 128
LATE = 3
HOLD = 0
HEAD = 0
LEAD = 0
AHEAD = 2
ORDER = "wrmwSHrmwrmwrmWwrmVwrmCDDwmDwm"


def plan(mesh, width, chunk):
    groups, subs = mesh.shape["grp"], mesh.shape["sub"]
    depth = 8 if subs >= 16 else 4
    chunks = width // chunk
    return dict(
        groups=groups,
        subs=subs,
        zs=depth,
        xs=subs // depth,
        chunk=chunk,
        chunks=chunks,
        per=chunk // LANES,
        blocks=width // LANES,
        order=ORDER,
        lead=LEAD,
        stride=max(1, subs // (width // LANES)),
        late=LATE,
        head=HEAD,
    )


def kernel(cfg, rs_hbm, s_hbm, g_hbm, k_hbm, idx_hbm, phase_hbm, table_hbm, sol_ref, res_ref, sc):
    groups, subs, zs, xs = cfg["groups"], cfg["subs"], cfg["zs"], cfg["xs"]
    chunk, chunks, per = cfg["chunk"], cfg["chunks"], cfg["per"]
    blocks, stride, late = cfg["blocks"], cfg["stride"], cfg["late"]
    early = chunks - late
    head = cfg["head"]
    face = rs_hbm.shape[0]
    prim = idx_hbm.shape[1]
    idx_ref, phase_ref, table_ref = sc["idx"], sc["phase"], sc["table"]
    g = lax.axis_index("grp")
    j = lax.axis_index("sub")
    x, z = j // zs, lax.rem(j, zs)
    right = lax.rem(j + 1, subs)
    left = lax.rem(j + subs - 1, subs)
    low = pl.ds(face, face)
    up = pl.ds(0, face)

    def remote(src, dst, ssem, rsem, where):
        return pltpu.make_async_remote_copy(
            src_ref=src, dst_ref=dst, send_sem=ssem, recv_sem=rsem, device_id=where, device_id_type=MESH
        )

    def drain(ref, sem):
        pltpu.make_async_copy(ref, ref, sem).wait()

    def cols(c):
        return pl.ds(pl.multiple_of(c * chunk, chunk), chunk)

    def load_rs(c):
        return pltpu.make_async_copy(rs_hbm.at[:, cols(c)], sc["rs"].at[c], sc["rs_sem"].at[c])

    load_g = pltpu.make_async_copy(g_hbm, sc["gm"], sc["mat_sem"].at[0])
    load_k = pltpu.make_async_copy(k_hbm, sc["km"], sc["mat_sem"].at[1])
    load_s = pltpu.make_async_copy(s_hbm, sc["sm"], sc["mat_sem"].at[2])

    def rb_copy(c):
        return remote(
            sc["ext"].at[c, low], sc["ext"].at[c, up], sc["rb_ss"].at[c], sc["rb_rs"].at[c], {"sub": right}
        )

    def v_copy(c):
        return remote(sc["v"].at[c, up], sc["vr"].at[c], sc["v_ss"].at[c], sc["v_rs"].at[c], {"sub": left})

    def zb_copy(c):
        return remote(
            sc["dir"].at[c, low], sc["dir"].at[c, up], sc["zb_ss"].at[c], sc["zb_rs"].at[c], {"sub": right}
        )

    def y_copy(c):
        return remote(sc["y"].at[c, up], sc["yr"].at[c], sc["y_ss"].at[c], sc["y_rs"].at[c], {"sub": left})

    small = [
        pltpu.make_async_copy(idx_hbm, idx_ref, sc["mat_sem"].at[3]),
        pltpu.make_async_copy(phase_hbm, phase_ref, sc["mat_sem"].at[4]),
        pltpu.make_async_copy(table_hbm, table_ref, sc["mat_sem"].at[5]),
    ]

    barrier = pltpu.get_barrier_semaphore()

    def greet(sem, where):
        pl.semaphore_signal(sem, inc=1, device_id=where, device_id_type=MESH)

    def greet_grp(d, carry):
        greet(barrier, {"grp": lax.rem(g + d, groups)})
        return carry

    def greet_sub(d, carry):
        greet(barrier, {"sub": lax.rem(j + 1 + lax.rem(d + subs // 3, subs - 1), subs)})
        return carry

    lax.fori_loop(1, subs, greet_sub, 0)
    lax.fori_loop(1, groups, greet_grp, 0)
    for c in range(chunks):
        load_rs(c).start()
    for load in small:
        load.start()
    load_g.start()
    load_k.start()
    load_s.start()

    def cast(c):
        load_rs(c).wait()
        sc["ext"][c, low, :] = sc["rs"][c].astype(BF16)

    def cast_all(c, carry):
        cast(c)
        return carry

    lax.fori_loop(0, chunks, cast_all, 0)

    def pick(c, carry):
        for k in range(prim):
            row = sc["rs"][c, pl.ds(idx_ref[0, k], 1), :]
            for h in range(per):
                sc["rc"][c * per + h, k : k + 1, :] = row[:, h * LANES : (h + 1) * LANES]
        return carry

    for load in small:
        load.wait()
    lax.fori_loop(0, chunks, pick, 0)

    def rc_copy(b):
        return remote(
            sc["rc"].at[b], sc["rcin"].at[j], sc["rc_ss"].at[b], sc["rc_rs"], {"sub": b * stride}
        )

    def rc_send(turn, carry):
        b = lax.rem(turn + j // stride, blocks)

        @pl.when(b * stride != j)
        def _():
            rc_copy(b).start()

        @pl.when(b * stride == j)
        def _():
            sc["rcin"][j] = sc["rc"][b]

        return carry

    load_g.wait()
    sc["gt"][...] = sc["gm"][...].T
    lane = lax.broadcasted_iota(jnp.int32, (4 * prim, face), 1)
    sub_i = lax.broadcasted_iota(jnp.int32, (4 * prim, face), 0)
    which = jnp.full((4 * prim, face), -1, jnp.int32)
    for k in range(prim):
        which = jnp.where(lax.rem(sub_i, prim) == k, idx_ref[0, k], which)
    hot = jnp.where((lane == which) & (sub_i < 3 * prim), 1.0, 0.0).astype(F32)
    sc["pt"][...] = hot.T.astype(BF16)
    labels = phase_ref[...]
    coef = jnp.zeros(labels.shape, F32)
    for k in range(table_ref.shape[1]):
        coef = jnp.where(labels == k, table_ref[0, k], coef)
    sc["coef"][...] = jnp.broadcast_to(coef, (LANES, face)).T
    sc["ra"][...] = jnp.zeros_like(sc["ra"])

    pl.semaphore_wait(barrier, groups - 1 + subs - 1)
    lax.fori_loop(0, blocks, rc_send, 0)
    for c in range(AHEAD):
        rb_copy(c).start()

    pt_copy = remote(sc["pt"], sc["ptl"], sc["el_ss"].at[0], sc["el_rs"].at[0], {"sub": right})
    el_copy = remote(sc["el"], sc["ell"], sc["el_ss"].at[1], sc["el_rs"].at[1], {"sub": right})
    if head:
        pt_copy.start()
    def first(c):
        u = jnp.dot(sc["gm"][...], sc["ext"][c], preferred_element_type=F32).astype(BF16)
        sc["v"][c] = jnp.dot(sc["gt"][...], u, preferred_element_type=F32).astype(BF16)
        v_copy(c).start()

    is_solver = (lax.rem(j, stride) == 0) & (j < blocks * stride)
    my_block = j // stride

    def h_copy(t):
        return remote(
            sc["hout"].at[t], sc["hin"].at[my_block], sc["h_ss"].at[t], sc["h_rs"], {"sub": t}
        )

    def solve():
        @pl.when(is_solver)
        def _():
            load_k.wait()
            drain(sc["rcin"].at[pl.ds(0, subs - 1)], sc["rc_rs"])
            rhs = sc["rcin"][...].reshape(subs * prim, LANES)
            h = jnp.dot(sc["km"][...], rhs, precision=lax.Precision.HIGHEST, preferred_element_type=F32)
            sc["hout"][...] = h.reshape(subs, prim, LANES)

        @pl.when(jnp.logical_not(is_solver))
        def _():
            load_k.wait()

    def give():
        @pl.when(is_solver)
        def _():
            def h_send(d, carry):
                h_copy(lax.rem(j + 1 + lax.rem(d + subs // 3, subs - 1), subs)).start()
                return carry

            lax.fori_loop(1, subs, h_send, 0)
            sc["hin"][my_block] = sc["hout"][j]

    cores = 2
    ys = groups // cores
    row, core = g // cores, lax.rem(g, cores)

    def g_copy(t):
        return remote(sc["hin"], sc["gin"].at[row], sc["g_ss"].at[t], sc["g_rs"], {"grp": t * cores + core})

    pair_copy = remote(
        sc["ysum"], sc["yother"], sc["p_ss"], sc["p_rs"], {"grp": row * cores + 1 - core}
    )

    def share():
        @pl.when(is_solver)
        def _():
            drain(sc["hin"].at[pl.ds(0, blocks - 1)], sc["h_rs"])

        @pl.when(jnp.logical_not(is_solver))
        def _():
            drain(sc["hin"], sc["h_rs"])

        for d in range(1, ys):
            g_copy(lax.rem(row + d, ys)).start()
        sc["gin"][row] = sc["hin"][...]

    def pair():
        if ys > 1:
            drain(sc["gin"].at[pl.ds(0, ys - 1)], sc["g_rs"])
        total = sc["gin"][0]
        for t in range(1, ys):
            total = total + sc["gin"][t]
        sc["ysum"][...] = total
        pair_copy.start()

    def split(e):
        hi = e.astype(BF16).astype(F32)
        rest = e - hi
        mid = rest.astype(BF16).astype(F32)
        tail = rest - mid
        return jnp.concatenate([hi, mid, tail, jnp.zeros_like(hi)], axis=0).astype(BF16)

    def correct():
        pair_copy.wait_recv()
        for b in range(blocks):
            total = sc["ysum"][b] + sc["yother"][b]
            e = sc["hin"][b] + total / groups
            c, h = divmod(b, per)
            sc["e3"][c, :, h * LANES : (h + 1) * LANES] = split(e)
            if c < head:
                sc["el"][b] = e
        if head:
            el_copy.start()

    def rows_to(ref, base, c, value):
        for h in range(per):
            ref[base + c * per + h] = value[:, h * LANES : (h + 1) * LANES]

    def low_copy(c):
        return remote(
            sc["v"].at[c, low], sc["dir"].at[c, up], sc["zb_ss"].at[c], sc["zb_rs"].at[c], {"sub": right}
        )

    def left_direction(c):
        stack = [split(sc["ell"][c * per + h]) for h in range(per)]
        fix = jnp.dot(sc["ptl"][...], jnp.concatenate(stack, axis=1), preferred_element_type=F32)
        both = sc["dir"][c, up, :].astype(F32) + sc["v"][c, up, :].astype(F32)
        sc["dir"][c, up, :] = (0.5 * both + fix).astype(BF16)

    def direction(c, send=True):
        v_copy(c).wait_recv()
        fix = jnp.dot(sc["pt"][...], sc["e3"][c], preferred_element_type=F32)
        both = sc["v"][c, low, :].astype(F32) + sc["vr"][c].astype(F32)
        zz = 0.5 * both + fix
        sc["dir"][c, low, :] = zz.astype(BF16)
        if send:
            zb_copy(c).start()
        rows_to(sc["ra"], 0, c, jnp.sum(sc["rs"][c] * zz, axis=0, keepdims=True))

    def wide_coef():
        return jnp.concatenate([sc["coef"][...]] * per, axis=1)

    def image(c, ref, base, send=True):
        y = jnp.dot(sc["sm"][...], sc["dir"][c], preferred_element_type=F32).astype(BF16)
        sc["y"][c] = y
        if send:
            y_copy(c).start()
        zf = sc["dir"][c, low, :].astype(F32)
        part = jnp.sum(sc["dir"][c].astype(F32) * sc["y"][c].astype(F32), axis=0, keepdims=True)
        part = part + jnp.sum(wide_coef() * zf * zf, axis=0, keepdims=True)
        rows_to(ref, base, c, part)

    def finish(c, carry):
        y_copy(c).wait_recv()
        alpha = jnp.concatenate([sc["alpha"][c * per + h] for h in range(per)], axis=1)
        zf = sc["dir"][c, low, :].astype(F32)
        q = sc["y"][c, low, :].astype(F32) + sc["yr"][c].astype(F32) + wide_coef() * zf
        sol_ref[:, cols(c)] = alpha * zf
        res_ref[:, cols(c)] = sc["rs"][c] - alpha * q
        return carry

    span = sc["ra"].shape[0] // groups

    def exchange(name, count, me, where, src_of):
        def copy(t):
            return remote(src_of(t), sc[name].at[me], sc[name + "_ss"].at[t], sc[name + "_rs"], where(t))

        def start(own):
            def go(d, carry):
                copy(lax.rem(me + 1 + lax.rem(d + count // 3, count - 1), count)).start()
                return carry

            lax.fori_loop(1, count, go, 0)
            sc[name][me] = own

        def end():
            drain(sc[name].at[pl.ds(0, count - 1)], sc[name + "_rs"])
            total = sc[name][0]
            for t in range(1, count):
                total = total + sc[name][t]
            return total

        def sent():
            def go(d, carry):
                copy(lax.rem(me + d, count)).wait_send()
                return carry

            lax.fori_loop(1, count, go, 0)

        return start, end, sent

    to_grp = lambda t: {"grp": t}
    to_x = lambda t: {"sub": t * zs + z}
    to_z = lambda t: {"sub": x * zs + t}
    a1 = exchange("a1", groups, g, to_grp, lambda t: sc["ra"].at[pl.ds(t * span, span)])
    a2 = exchange("a2", xs, x, to_x, lambda t: sc["a2o"])
    a3 = exchange("a3", zs, z, to_z, lambda t: sc["a3o"])
    a4 = exchange("a4", groups, g, to_grp, lambda t: sc["a4o"])
    b1 = exchange("b1", groups, g, to_grp, lambda t: sc["rbt"])
    b2 = exchange("b2", subs, j, lambda t: {"sub": t}, lambda t: sc["b2o"])

    def hop(before, after, name):
        total = before[1]()
        sc[name][...] = total
        after[0](total)

    count = {"w": 0, "m": 0, "r": AHEAD, "L": 0, "D": 0}
    actions = {
        "w": lambda c: rb_copy(c).wait_recv(),
        "m": first,
        "r": lambda c: rb_copy(c).start(),
        "L": lambda c: low_copy(c).start(),
        "D": lambda c: direction(c, send=c >= head),
    }
    steps = {"S": solve, "H": give, "W": share, "V": pair, "C": correct}
    lead = cfg["lead"]
    for step in cfg["order"]:
        if step in steps:
            steps[step]()
        else:
            actions[step](count[step])
            count[step] += 1
    load_s.wait()
    base = chunks * per

    ready = max(head, count["D"])
    for c in range(ready, min(chunks, ready + lead)):
        direction(c)
    ready = min(chunks, ready + lead)
    if head:
        pt_copy.wait_recv()
        el_copy.wait_recv()
    for c in range(chunks):
        if c == early:
            a1[0](sc["ra"][pl.ds(g * span, span)])
        if c == early + 1:
            hop(a1, a2, "a2o")
        if c == early + 2:
            hop(a2, a3, "a3o")
        if c < head and c >= count["D"]:
            direction(c, send=False)
        if ready < chunks and c >= head:
            direction(ready)
            ready += 1
        zb_copy(c).wait_recv()
        if c < head:
            left_direction(c)
        if ready < chunks and c < head:
            direction(ready)
            ready += 1
        if c < early:
            image(c, sc["ra"], base)
        else:
            image(c, sc["rbt"], -early * per, send=c < chunks - HOLD)
    b1[0](sc["rbt"][...])
    if late < 3:
        hop(a2, a3, "a3o")
    hop(b1, b2, "b2o")
    for c in range(chunks - HOLD, chunks):
        y_copy(c).start()
    hop(a3, a4, "a4o")
    drain(sc["a4"].at[pl.ds(0, groups - 1)], sc["a4_rs"])
    for r in range(early * per):
        n, d = r, base + r
        sc["alpha"][r] = sc["a4"][n // span, n % span] / sc["a4"][d // span, d % span]
    lax.fori_loop(0, early, finish, 0)
    last = b2[1]()
    for r in range(late * per):
        n = early * per + r
        sc["alpha"][n] = sc["a4"][n // span, n % span] / last[r]
    lax.fori_loop(early, chunks, finish, 0)

    if head:
        pt_copy.wait_send()
        el_copy.wait_send()

    def drain_streams(c, carry):
        rb_copy(c).wait_send()
        v_copy(c).wait_send()
        zb_copy(c).wait_send()
        y_copy(c).wait_send()
        return carry

    lax.fori_loop(0, chunks, drain_streams, 0)

    def drain_rc(b, carry):
        @pl.when(b * stride != j)
        def _():
            rc_copy(b).wait_send()

        return carry

    lax.fori_loop(0, blocks, drain_rc, 0)

    @pl.when(is_solver)
    def _():
        def drain_h(d, carry):
            h_copy(lax.rem(j + d, subs)).wait_send()
            return carry

        lax.fori_loop(1, subs, drain_h, 0)

    for d in range(1, ys):
        g_copy(lax.rem(row + d, ys)).wait_send()
    pair_copy.wait_send()
    for stage in (a1, a2, a3, a4, b1, b2):
        stage[2]()


def write_out(sol_ref, res_ref, sol_hbm, res_hbm, sems):
    copies = [
        pltpu.make_async_copy(sol_ref, sol_hbm, sems.at[0]),
        pltpu.make_async_copy(res_ref, res_hbm, sems.at[1]),
    ]
    for copy in copies:
        copy.start()
    for copy in copies:
        copy.wait()


def scratch(cfg, face, prim, phases):
    n, chunk, per = cfg["chunks"], cfg["chunk"], cfg["per"]
    groups, subs, xs, zs, blocks = cfg["groups"], cfg["subs"], cfg["xs"], cfg["zs"], cfg["blocks"]
    rows_a = (2 * n - cfg["late"]) * per
    span = -(-rows_a // groups)
    rows_b = cfg["late"] * per
    vm, dma = pltpu.VMEM, pltpu.SemaphoreType.DMA
    out = dict(
        rs=vm((n, face, chunk), F32),
        ext=vm((n, 2 * face, chunk), BF16),
        v=vm((n, 2 * face, chunk), BF16),
        vr=vm((n, face, chunk), BF16),
        dir=vm((n, 2 * face, chunk), BF16),
        y=vm((n, 2 * face, chunk), BF16),
        yr=vm((n, face, chunk), BF16),
        ptl=vm((face, 4 * prim), BF16),
        el=vm((max(cfg["head"], 1) * per, prim, LANES), F32),
        ell=vm((max(cfg["head"], 1) * per, prim, LANES), F32),
        el_ss=dma((2,)),
        el_rs=dma((2,)),
        idx=pltpu.SMEM((1, prim), jnp.int32),
        phase=vm((1, face), jnp.int32),
        table=pltpu.SMEM((1, phases), F32),
        gm=vm((2 * face, 2 * face), BF16),
        gt=vm((2 * face, 2 * face), BF16),
        sm=vm((2 * face, 2 * face), BF16),
        km=vm((subs * prim, subs * prim), F32),
        pt=vm((face, 4 * prim), BF16),
        coef=vm((face, LANES), F32),
        rc=vm((blocks, prim, LANES), F32),
        rcin=vm((subs, prim, LANES), F32),
        hout=vm((subs, prim, LANES), F32),
        hin=vm((blocks, prim, LANES), F32),
        gin=vm((groups // 2, blocks, prim, LANES), F32),
        ysum=vm((blocks, prim, LANES), F32),
        yother=vm((blocks, prim, LANES), F32),
        e3=vm((n, 4 * prim, chunk), BF16),
        alpha=vm((n * per, 1, LANES), F32),
        ra=vm((span * groups, 1, LANES), F32),
        rbt=vm((rows_b, 1, LANES), F32),
        a1=vm((groups, span, 1, LANES), F32),
        a2=vm((xs, span, 1, LANES), F32),
        a3=vm((zs, span, 1, LANES), F32),
        a4=vm((groups, span, 1, LANES), F32),
        a2o=vm((span, 1, LANES), F32),
        a3o=vm((span, 1, LANES), F32),
        a4o=vm((span, 1, LANES), F32),
        b1=vm((groups, rows_b, 1, LANES), F32),
        b2=vm((subs, rows_b, 1, LANES), F32),
        b2o=vm((rows_b, 1, LANES), F32),
        rs_sem=dma((n,)),
        mat_sem=dma((6,)),
        rc_ss=dma((blocks,)),
        rc_rs=dma(()),
        h_ss=dma((subs,)),
        h_rs=dma(()),
        g_ss=dma((groups // 2,)),
        p_ss=dma(()),
        p_rs=dma(()),
        g_rs=dma(()),
    )
    for name in ("rb", "v", "zb", "y"):
        out[name + "_ss"] = dma((n,))
        out[name + "_rs"] = dma((n,))
    for name, count in (("a1", groups), ("a2", xs), ("a3", zs), ("a4", groups), ("b1", groups), ("b2", subs)):
        out[name + "_ss"] = dma((count,))
        out[name + "_rs"] = dma(())
    return out


def solution(mesh, chunk=CHUNK):
    def body(right_side, schur, inv_factor, coarse_inverse, primal_index, phase, phase_coef):
        face, width = right_side.shape
        cfg = plan(mesh, width, chunk)
        shapes = scratch(cfg, face, primal_index.shape[1], phase_coef.shape[0])
        keys = list(shapes)

        def wrapped(*refs):
            kernel(cfg, *refs[:9], dict(zip(keys, refs[9:])))

        hbm = pl.BlockSpec(memory_space=pltpu.HBM)
        vmem = pl.BlockSpec(memory_space=pltpu.VMEM)
        out = jax.ShapeDtypeStruct((face, width), F32)
        operands = (right_side, schur, inv_factor, coarse_inverse, primal_index)
        operands += (phase.reshape(1, face), phase_coef.reshape(1, -1))
        held = pltpu.VMEM((face, width), F32)
        results = pl.pallas_call(
            wrapped,
            out_shape=(held, held),
            in_specs=[hbm] * 7,
            out_specs=(vmem, vmem),
            scratch_shapes=[shapes[k] for k in keys],
            compiler_params=pltpu.CompilerParams(
                collective_id=0, has_side_effects=True, vmem_limit_bytes=44 * 1024 * 1024
            ),
            name="bddc_step",
        )(*[pltpu.with_memory_space_constraint(a, pltpu.HBM) for a in operands])
        return pl.pallas_call(
            write_out,
            out_shape=(out, out),
            in_specs=[vmem, vmem],
            out_specs=(hbm, hbm),
            scratch_shapes=[pltpu.SemaphoreType.DMA((2,))],
            compiler_params=pltpu.CompilerParams(vmem_limit_bytes=1024 * 1024),
            name="write_out",
        )(*results)

    both = ("grp", "sub")
    in_specs = (
        P(both, None),
        P(both, None),
        P(both, None),
        P("grp", None),
        P(both, None),
        P(both),
        P(),
    )
    out_specs = (P(both, None), P(both, None))
    return jax.shard_map(body, mesh=mesh, in_specs=in_specs, out_specs=out_specs, check_vma=False)
```
